32 devices in a mesh: groups: 2 (over x), blk: 16 (over z, y, core).
Axes of the slice: x: 2, y: 2, z: 4, core: 2. Of those that a mesh axis runs over, the one named last changes fastest.
Arguments:
- embed: bfloat16 [16384, 1024], P(('groups', 'blk')), parts along dimension 0, may hold values from -6 to 6
- owner: int32 [16384, 1], P(('groups', 'blk')), parts along dimension 0, may hold values from 0 to 15; in each aligned block of 512 rows (0 to 511, 512 to 1023, ...) at most 64 rows name the same one
- near: int32 [32], P('groups'), parts along dimension 0, may hold values from 0 to 1
Outputs:
- density: float32 [16384], P(('groups', 'blk')), parts along dimension 0
The draws below stay inside these ranges and needn't reach their ends.
There are 2 independent parts, one for each index of `groups`. The reference program is written for one: setup_inputs(seed, part) draws one part's arguments, and reference() takes and returns one part's arrays. A program takes and returns all parts, laid end to end along the dimension named above; each array names one. Nothing has to cross between parts.
Inputs may be any that keep to these rules, and one draw needn't show every extreme that they name: Among the rows of one device no owner is named more than 64 times, a bound that some block reaches.
All inputs are finite; a program needn't handle non-finite values.
Results may differ from the reference program's by a relative error of at most 0.0003.
Values may be sent and summed in bfloat16 or wider, within the bound.
No kernel may reach another device: no remote copies, remote signals or barrier semaphores. Data moves between devices by JAX's collectives and lax.ppermute only.
A program may use at most 64 MiB of HBM per device.

```python
import math
import jax
import jax.numpy as jnp
import numpy as np
from jax import lax

D = 1024
ROWS_DEV = 512
CAP = 64
ROWS = 8192
N_BLK = 16


def place_ends(array, key, smallest, largest):
    dims = array.shape
    place = [jax.random.randint(jax.random.fold_in(key, axis), (), 0, dims[axis]) for axis in range(len(dims))]
    array = array.at[tuple(place)].set(smallest)
    longest = dims.index(max(dims))
    place[longest] = (place[longest] + 1) % dims[longest]
    return array.at[tuple(place)].set(largest)


def shard_levels(own_key, extent, cuts, least, high):
    gain = 1.0
    for axis_at, blocks in cuts:
        steps = jax.random.uniform(jax.random.fold_in(jax.random.fold_in(own_key, 6), axis_at), (blocks,), jnp.float32, least / len(cuts), high / len(cuts))
        gain = gain * jnp.repeat(jnp.exp(steps), extent[axis_at] // blocks).reshape((-1,) + (1,) * (len(extent) - 1 - axis_at))
    return gain


def shared_out(stream_key, own, number, rows, count, top, most, lean):
    order = jax.random.permutation(stream_key, count)
    heavy_load, usual = portions_of(count, rows * top, most, lean, True), portions_of(count, rows * top, most, lean, False)
    places = jnp.arange(count)

    def named(lengths, turn):
        used = int((lengths > 0).sum())
        fixed = max(1, used // 4)
        passed = fixed + (places - fixed + turn * (used - fixed)) % max(1, count - fixed)
        return jnp.zeros((count,), jnp.int32).at[order[jnp.where(places < fixed, places, passed)]].set(jnp.asarray(lengths, jnp.int32))

    lengths = jnp.where(number % 4 == 0, named(heavy_load, number // 4), named(usual, number - number // 4 - 1))
    mixed = jax.random.permutation(jax.random.fold_in(own, 3), count)
    donor, sink = mixed[0:count // 2 * 2:2], mixed[1:count // 2 * 2:2]
    margin = jnp.minimum(lengths[donor] - 1, most - lengths[sink]) // 2
    margin = jnp.where((donor == order[0]) | (sink == order[0]) | (lengths[sink] == 0), 0, jnp.maximum(margin, 0))
    passed = jax.random.randint(jax.random.fold_in(own, 4), (count // 2,), 0, 1 << 20) % (margin + 1)
    lengths = lengths.at[donor].add(-passed).at[sink].add(passed)
    members = jnp.searchsorted(jnp.cumsum(lengths), jnp.arange(rows * top), side="right").astype(jnp.int32)
    listing = members.reshape(top, rows).T
    listing = listing[jax.random.permutation(jax.random.fold_in(own, 1), rows)]
    turn = jax.random.randint(jax.random.fold_in(own, 2), (rows, 1), 0, top)
    return jnp.take_along_axis(listing, (jnp.arange(top)[None, :] + turn) % top, axis=1)


def portions_of(count, total, most, skew, full):
    portions = [(1 << 20) // math.isqrt(standing ** skew) + 1 for standing in range(1, count + 1)]
    largest = most if full else min(most, max(-(-total // count), total * portions[0] // sum(portions)))
    least = 1 if total - largest >= count - 1 else 0
    counts, surplus = [largest] + [least] * (count - 1), total - largest - least * (count - 1)
    while surplus > 0:
        movable = [i for i in range(1, count) if counts[i] < largest] or [i for i in range(1, count) if counts[i] < most]
        whole, budget = sum([portions[i] for i in movable]), surplus
        for i in movable:
            addition = min(most - counts[i], max(1, budget * portions[i] // whole), surplus)
            counts[i] = counts[i] + addition
            surplus = surplus - addition
    return np.array(counts)


def gaussian(key, dims, deviation, bound, pieces=(), held_as=jnp.bfloat16):
    drawn = deviation * jax.random.normal(key, dims, jnp.float32)
    if pieces:
        drawn = drawn * shard_levels(key, dims, pieces, -0.22, 0.18)
    return jnp.clip(drawn, -bound, bound).astype(held_as)


def setup_inputs(seed: int = 0, part: int = 0) -> dict:
    streams_of = jax.random.split(jax.random.key(seed), 4)
    part_keys = jax.random.split(jax.random.fold_in(streams_of[3], part), 4)
    embed = gaussian(part_keys[0], (ROWS, D), 1.0, 6.0, ((0, 16),))
    owner_keys = jax.random.split(jax.random.fold_in(part_keys[1], 1), ROWS // ROWS_DEV)
    owner_turns = jax.random.permutation(jax.random.fold_in(part_keys[1], 3), ROWS // ROWS_DEV)
    owner = jax.vmap(lambda own, number: shared_out(jax.random.fold_in(part_keys[1], 2), own, number, ROWS_DEV, N_BLK, 1, CAP, 2))(owner_keys, owner_turns).reshape((ROWS, 1))
    near = place_ends(jax.random.randint(part_keys[2], (N_BLK,), 0, 2), jax.random.fold_in(part_keys[2], 1), 0, 1).astype(jnp.int32)
    return dict(embed=embed, owner=owner, near=near)


def pair_terms(a_rows, a_used, b_rows, b_used, same, factor):
    sim = jnp.dot(a_rows.astype(jnp.float32), b_rows.astype(jnp.float32).T, precision=lax.Precision.HIGHEST)
    weight = a_used[:, None] * b_used[None, :] * factor
    if same:
        count = a_rows.shape[0]
        weight = jnp.where(jnp.arange(count)[:, None] == jnp.arange(count)[None, :], jnp.float32(0.0), weight)
    return weight * jnp.exp(16.0 * sim)

def reference(embed, owner, near):
    values = embed.astype(jnp.float32)
    scale = lax.rsqrt(lax.optimization_barrier(jnp.mean(values * values, axis=-1, keepdims=True)) + 1e-06) / jnp.sqrt(jnp.float32(D))
    unit = (values * scale).astype(jnp.bfloat16)
    owned = owner[:, 0].astype(jnp.int32)
    onehot = (owned[:, None] == jnp.arange(N_BLK, dtype=jnp.int32)[None, :]).astype(jnp.int32)
    blocks = onehot.reshape(N_BLK, ROWS_DEV, N_BLK)
    rank = lax.optimization_barrier(jnp.sum((jnp.cumsum(blocks, axis=1) - blocks) * blocks, axis=-1)).reshape(ROWS).astype(jnp.int32)
    source = (jnp.arange(ROWS, dtype=jnp.int32) // ROWS_DEV).astype(jnp.int32)
    position = (source * CAP + rank).astype(jnp.int32)
    slots = N_BLK * CAP
    buffer = jnp.zeros((N_BLK, slots, D), jnp.bfloat16).at[owned, position].set(unit)
    used = jnp.zeros((N_BLK, slots), jnp.float32).at[owned, position].set(jnp.float32(1.0))
    nearby = near.astype(jnp.int32)

    def per_owner(index):
        nexts = (index + 1) % N_BLK
        factor = 0.5 * (nearby[index] == 1).astype(jnp.float32) + 0.5 * (nearby[nexts] == 0).astype(jnp.float32)
        self_terms = pair_terms(buffer[index], used[index], buffer[index], used[index], True, jnp.float32(1.0))
        cross = pair_terms(buffer[index], used[index], buffer[nexts], used[nexts], False, factor)
        return (lax.optimization_barrier(jnp.sum(self_terms, axis=1)), lax.optimization_barrier(jnp.sum(cross, axis=1)), lax.optimization_barrier(jnp.sum(cross, axis=0)))
    self_rows, cross_rows, cross_cols = lax.map(per_owner, jnp.arange(N_BLK, dtype=jnp.int32))
    totals = self_rows + cross_rows + jnp.roll(cross_cols, 1, axis=0)
    scores = jnp.log1p(totals)
    return scores[owned, position]
```

```python
import functools

import jax
import jax.numpy as jnp
from jax import lax
from jax.experimental import pallas as pl
from jax.experimental.pallas import tpu as pltpu
from jax.sharding import PartitionSpec as P

STRIP = 256


def unit_rows(values):
    values = values.astype(jnp.float32)
    width = values.shape[-1]
    scale = lax.rsqrt(jnp.mean(values * values, axis=-1, keepdims=True) + 1e-06) / jnp.sqrt(
        jnp.float32(width)
    )
    return (values * scale).astype(jnp.bfloat16)


def decode(code, clusters):
    own = code // 2
    near = code - 2 * own
    nearest = own + 2 * near - 1
    nearest = jnp.where(nearest < 0, nearest + clusters, nearest)
    nearest = jnp.where(nearest >= clusters, nearest - clusters, nearest)
    return own, nearest


def as_column(row):
    return jnp.transpose(jnp.broadcast_to(row, (128, row.shape[1])))


def terms(a_unit, b_unit, a_own, a_near, b_own, b_near):
    sim = lax.dot_general(
        a_unit, b_unit, (((1,), (1,)), ((), ())), preferred_element_type=jnp.float32
    )
    value = jnp.exp(16.0 * sim)
    wide = value.shape[1] // 128
    a_own, a_near = jnp.tile(a_own, (1, wide)), jnp.tile(a_near, (1, wide))
    near = jnp.where(a_near == b_own, value, 0.0) + jnp.where(a_own == b_near, value, 0.0)
    return jnp.where(a_own == b_own, value, 0.0) + 0.5 * near


def lanes_added(x):
    out = x[:, :128]
    for at in range(128, x.shape[1], 128):
        out = out + x[:, at : at + 128]
    return out


def as_row(x):
    return jnp.sum(jnp.transpose(x), axis=0, keepdims=True)


def normalise(source, target):
    rows = source.shape[0]
    for at in range(0, rows, STRIP):
        target[at : at + STRIP, :] = unit_rows(source[at : at + STRIP, :])


def own_kernel(clusters, mine, other, mine_code, other_code, mine_unit, other_unit, sums):
    normalise(mine, mine_unit)
    normalise(other, other_unit)
    rows = mine.shape[0]
    a_own, a_near = [as_column(v) for v in decode(mine_code[...], clusters)]
    strips = []
    for at in range(0, rows, STRIP):
        total = jnp.zeros((STRIP, 128), jnp.float32)
        for same, unit, code in ((True, mine_unit, mine_code), (False, other_unit, other_code)):
            b_own, b_near = decode(code[...], clusters)
            value = terms(
                mine_unit[at : at + STRIP, :],
                unit[...],
                a_own[at : at + STRIP],
                a_near[at : at + STRIP],
                b_own,
                b_near,
            )
            if same:
                place = lax.broadcasted_iota(jnp.int32, value.shape, 0) + at
                value = jnp.where(
                    place == lax.broadcasted_iota(jnp.int32, value.shape, 1), 0.0, value
                )
            total = total + lanes_added(value)
        strips.append(as_row(total))
    sums[...] = jnp.concatenate(strips, axis=1)


def pair_kernel(clusters, ready, raw, *refs):
    blocks = ready + raw
    a_rows, refs = refs[:blocks], refs[blocks:]
    a_codes, refs = refs[:blocks], refs[blocks:]
    b_rows, b_code, refs = refs[0], refs[1], refs[2:]
    a_units, refs = refs[:raw], refs[raw:]
    a_sums, b_sums, b_unit = refs
    normalise(b_rows, b_unit)
    b_own, b_near = decode(b_code[...], clusters)
    rows = b_rows.shape[0]
    b_total = jnp.zeros((8, rows), jnp.float32)
    for block in range(blocks):
        a_own, a_near = [as_column(v) for v in decode(a_codes[block][...], clusters)]
        unit = a_rows[block]
        if block >= ready:
            unit = a_units[block - ready]
            normalise(a_rows[block], unit)
        for at in range(0, rows, STRIP):
            value = terms(
                unit[at : at + STRIP, :],
                b_unit[...],
                a_own[at : at + STRIP],
                a_near[at : at + STRIP],
                b_own,
                b_near,
            )
            a_sums[block : block + 1, at : at + STRIP] = as_row(lanes_added(value))
            b_total = b_total + jnp.sum(value.reshape(STRIP // 8, 8, rows), axis=0)
    b_sums[...] = jnp.sum(b_total, axis=0, keepdims=True)


def vmem(count):
    return [pl.BlockSpec(memory_space=pltpu.VMEM)] * count


def cost(tiles, rows, width):
    return pl.CostEstimate(
        flops=2 * tiles * rows * rows * width,
        bytes_accessed=4 * rows * width,
        transcendentals=tiles * rows * rows,
    )


def own_terms(clusters, mine, other, mine_code, other_code):
    rows, width = mine.shape
    unit = jax.ShapeDtypeStruct((rows, width), jnp.bfloat16)
    return pl.pallas_call(
        functools.partial(own_kernel, clusters),
        out_shape=(unit, unit, jax.ShapeDtypeStruct((1, rows), jnp.float32)),
        in_specs=vmem(4),
        out_specs=vmem(3),
        compiler_params=pltpu.CompilerParams(vmem_limit_bytes=40 << 20),
        cost_estimate=cost(2, rows, width),
        name="own_terms",
    )(mine, other, mine_code, other_code)


def pair_sums(clusters, ready, raw, a_codes, b_rows, b_code):
    rows, width = b_rows.shape
    blocks = len(ready) + len(raw)
    unit = jax.ShapeDtypeStruct((rows, width), jnp.bfloat16)
    outs = pl.pallas_call(
        functools.partial(pair_kernel, clusters, len(ready), len(raw)),
        out_shape=(unit,) * len(raw)
        + (
            jax.ShapeDtypeStruct((blocks, rows), jnp.float32),
            jax.ShapeDtypeStruct((1, rows), jnp.float32),
        ),
        in_specs=vmem(2 * blocks + 2),
        out_specs=vmem(len(raw) + 2),
        scratch_shapes=[pltpu.VMEM((rows, width), jnp.bfloat16)],
        compiler_params=pltpu.CompilerParams(vmem_limit_bytes=40 << 20),
        cost_estimate=cost(blocks, rows, width),
        name="pair_sums",
    )(*ready, *raw, *a_codes, b_rows, b_code)
    a_sums = outs[-2]
    return outs[: len(raw)], [a_sums[i : i + 1] for i in range(blocks)], outs[-1]


def per_device(embed, owner, near):
    rows = embed.shape[0]
    clusters = near.shape[0]
    chips = lax.axis_size("blk") // 2
    hops = chips // 4
    order = list(range(0, chips, 2)) + list(range(chips - 1, 0, -2))

    def along(block, distance, crossed=lambda place: 0):
        route = []
        for place in range(chips):
            there = (place + distance) % chips
            for core in range(2):
                route.append((2 * order[place] + core, 2 * order[there] + (core ^ crossed(there))))
        return lax.ppermute(block, "blk", route)

    def other_core(block):
        return lax.ppermute(block, "blk", [(i, i ^ 1) for i in range(2 * chips)])

    def late(place):
        return int(place >= chips // 2)

    owned = owner[:, 0]
    names = jnp.arange(clusters, dtype=jnp.int32)
    nearby = jnp.sum(
        jnp.where(owned[None, :] == names[:, None], near[:, None], 0), axis=0, keepdims=True
    )
    code = 2 * owned[None, :] + nearby

    behind, ahead = [embed], [embed]
    behind_code, ahead_code = [code], [code]
    for hop in range(1, hops + 1):
        crossed = late if hop == hops else lambda place: 0
        behind.append(along(behind[-1], 1))
        ahead.append(along(ahead[-1], -1, crossed))
        behind_code.append(along(behind_code[-1], 1))
        ahead_code.append(along(ahead_code[-1], -1, crossed))
    spare = [other_core(block) for block in behind[:hops]]
    spare_code = [other_core(block) for block in behind_code[:hops]]

    unit, spare_unit, total = own_terms(clusters, embed, spare[0], code, spare_code[0])
    units = [unit, spare_unit]
    codes = [code, spare_code[0]]
    sums = None
    for hop in range(1, hops + 1):
        last = hop == hops
        raw = [behind[hop]] if last else [behind[hop], spare[hop]]
        raw_codes = [behind_code[hop]] if last else [behind_code[hop], spare_code[hop]]
        raw_units, a_sums, b_sums = pair_sums(
            clusters, units, raw, codes + raw_codes, ahead[hop], ahead_code[hop]
        )
        if sums is not None:
            a_sums[0], a_sums[1] = a_sums[0] + sums[0], a_sums[1] + sums[1]
        done = a_sums[0] + other_core(a_sums[1])
        total = total + (done if hop == 1 else along(done, 1 - hop))
        if last:
            route = []
            for place in range(chips):
                there = (place + hop) % chips
                for core in range(2):
                    route.append(
                        (2 * order[place] + core, 2 * order[there] + (core ^ late(place)))
                    )
            total = total + lax.ppermute(b_sums, "blk", route)
            total = total + along(a_sums[2], -hop)
        else:
            total = total + along(b_sums, hop)
            sums = a_sums[2:]
            units, codes = list(raw_units), raw_codes
    return jnp.log1p(total)[0]


def solution(mesh):
    return jax.shard_map(
        per_device,
        mesh=mesh,
        in_specs=(P(("groups", "blk"), None), P(("groups", "blk"), None), P("groups")),
        out_specs=P(("groups", "blk")),
        check_vma=False,
    )
```

```python
import functools

import jax
import jax.numpy as jnp
from jax import lax
from jax.experimental import pallas as pl
from jax.experimental.pallas import tpu as pltpu
from jax.sharding import PartitionSpec as P

STRIP = 256
META = 16


def unit_rows(values):
    values = values.astype(jnp.float32)
    width = values.shape[-1]
    scale = lax.rsqrt(jnp.mean(values * values, axis=-1, keepdims=True) + 1e-06) / jnp.sqrt(
        jnp.float32(width)
    )
    return (values * scale).astype(jnp.bfloat16)


def decode(code, clusters):
    own = code // 2
    near = code - 2 * own
    nearest = own + 2 * near - 1
    nearest = jnp.where(nearest < 0, nearest + clusters, nearest)
    nearest = jnp.where(nearest >= clusters, nearest - clusters, nearest)
    return own, nearest


def as_column(row):
    return jnp.transpose(jnp.broadcast_to(row, (128, row.shape[1])))


def terms(a_unit, b_unit, a_own, a_near, b_own, b_near):
    sim = lax.dot_general(
        a_unit, b_unit, (((1,), (1,)), ((), ())), preferred_element_type=jnp.float32
    )
    value = jnp.exp(16.0 * sim)
    wide = value.shape[1] // 128
    a_own, a_near = jnp.tile(a_own, (1, wide)), jnp.tile(a_near, (1, wide))
    near = jnp.where(a_near == b_own, value, 0.0) + jnp.where(a_own == b_near, value, 0.0)
    return jnp.where(a_own == b_own, value, 0.0) + 0.5 * near


def lanes_added(x):
    out = x[:, :128]
    for at in range(128, x.shape[1], 128):
        out = out + x[:, at : at + 128]
    return out


def as_row(x):
    return jnp.sum(jnp.transpose(x), axis=0, keepdims=True)


def codes_of(ref, clusters):
    rows = ref.shape[0] - META
    code = ref[rows:, :rows].astype(jnp.float32)[:1].astype(jnp.int32)
    return decode(code, clusters)


def pack_kernel(clusters, embed, owner, near, out, held, sems):
    rows = embed.shape[0]
    copies = []
    for i, at in enumerate(range(0, rows, STRIP // 2)):
        part = pl.ds(at, STRIP // 2)
        copies.append(pltpu.make_async_copy(embed.at[part], held.at[part], sems.at[i]))
        copies[-1].start()
    own = owner[...]
    near_own = jnp.zeros_like(own)
    for name in range(clusters):
        near_own = jnp.where(own == name, near[name], near_own)
    code = (2 * own + near_own).astype(jnp.float32)
    out[rows:, :] = jnp.zeros((META, out.shape[1]), jnp.bfloat16)
    out[rows:, :rows] = jnp.broadcast_to(code, (META, rows)).astype(jnp.bfloat16)
    for i, at in enumerate(range(0, rows, STRIP // 2)):
        copies[i].wait()
        out[at : at + STRIP // 2, :] = unit_rows(held[at : at + STRIP // 2, :])


def own_kernel(clusters, mine, other, sums):
    rows = mine.shape[0] - META
    a_own, a_near = [as_column(v) for v in codes_of(mine, clusters)]
    strips = []
    for at in range(0, rows, STRIP):
        total = jnp.zeros((STRIP, 128), jnp.float32)
        for same, block in ((True, mine), (False, other)):
            b_own, b_near = codes_of(block, clusters)
            value = terms(
                mine[at : at + STRIP, :],
                block[:rows, :],
                a_own[at : at + STRIP],
                a_near[at : at + STRIP],
                b_own,
                b_near,
            )
            if same:
                place = lax.broadcasted_iota(jnp.int32, value.shape, 0) + at
                value = jnp.where(
                    place == lax.broadcasted_iota(jnp.int32, value.shape, 1), 0.0, value
                )
            total = total + lanes_added(value)
        strips.append(as_row(total))
    sums[...] = jnp.concatenate(strips, axis=1)


def pair_kernel(clusters, blocks, *refs):
    a_blocks, b, a_sums, b_sums = refs[:blocks], refs[blocks], refs[-2], refs[-1]
    b_own, b_near = codes_of(b, clusters)
    rows = b.shape[0] - META
    b_total = jnp.zeros((8, rows), jnp.float32)
    for number, block in enumerate(a_blocks):
        a_own, a_near = [as_column(v) for v in codes_of(block, clusters)]
        for at in range(0, rows, STRIP):
            value = terms(
                block[at : at + STRIP, :],
                b[:rows, :],
                a_own[at : at + STRIP],
                a_near[at : at + STRIP],
                b_own,
                b_near,
            )
            a_sums[number : number + 1, at : at + STRIP] = as_row(lanes_added(value))
            b_total = b_total + jnp.sum(value.reshape(STRIP // 8, 8, rows), axis=0)
    b_sums[...] = jnp.sum(b_total, axis=0, keepdims=True)


def vmem(count):
    return [pl.BlockSpec(memory_space=pltpu.VMEM)] * count


def cost(tiles, rows, width):
    return pl.CostEstimate(
        flops=2 * tiles * rows * rows * width,
        bytes_accessed=4 * rows * width,
        transcendentals=tiles * rows * rows,
    )


def packed(clusters, embed, owner, near):
    rows, width = embed.shape
    return pl.pallas_call(
        functools.partial(pack_kernel, clusters),
        out_shape=jax.ShapeDtypeStruct((rows + META, width), jnp.bfloat16),
        in_specs=[
            pl.BlockSpec(memory_space=pl.ANY),
            pl.BlockSpec(memory_space=pltpu.VMEM),
            pl.BlockSpec(memory_space=pltpu.SMEM),
        ],
        out_specs=pl.BlockSpec(memory_space=pltpu.VMEM),
        scratch_shapes=[
            pltpu.VMEM((rows, width), jnp.bfloat16),
            pltpu.SemaphoreType.DMA((2 * rows // STRIP,)),
        ],
        compiler_params=pltpu.CompilerParams(vmem_limit_bytes=40 << 20),
        cost_estimate=cost(0, rows, width),
        name="packed",
    )(embed, owner, near)


def own_terms(clusters, mine, other):
    rows, width = mine.shape[0] - META, mine.shape[1]
    return pl.pallas_call(
        functools.partial(own_kernel, clusters),
        out_shape=jax.ShapeDtypeStruct((1, rows), jnp.float32),
        in_specs=vmem(2),
        out_specs=pl.BlockSpec(memory_space=pltpu.VMEM),
        compiler_params=pltpu.CompilerParams(vmem_limit_bytes=40 << 20),
        cost_estimate=cost(2, rows, width),
        name="own_terms",
    )(mine, other)


def pair_sums(clusters, a_blocks, b):
    rows, width = b.shape[0] - META, b.shape[1]
    blocks = len(a_blocks)
    a_sums, b_sums = pl.pallas_call(
        functools.partial(pair_kernel, clusters, blocks),
        out_shape=(
            jax.ShapeDtypeStruct((blocks, rows), jnp.float32),
            jax.ShapeDtypeStruct((1, rows), jnp.float32),
        ),
        in_specs=vmem(blocks + 1),
        out_specs=vmem(2),
        compiler_params=pltpu.CompilerParams(vmem_limit_bytes=40 << 20),
        cost_estimate=cost(blocks, rows, width),
        name="pair_sums",
    )(*a_blocks, b)
    return [a_sums[i : i + 1] for i in range(blocks)], b_sums


def per_device(embed, owner, near):
    rows = embed.shape[0]
    clusters = near.shape[0]
    chips = lax.axis_size("blk") // 2
    hops = chips // 4
    order = list(range(0, chips, 2)) + list(range(chips - 1, 0, -2))

    def along(block, distance, crossed=lambda place: 0):
        route = []
        for place in range(chips):
            there = (place + distance) % chips
            for core in range(2):
                route.append((2 * order[place] + core, 2 * order[there] + (core ^ crossed(there))))
        return lax.ppermute(block, "blk", route)

    def other_core(block):
        return lax.ppermute(block, "blk", [(i, i ^ 1) for i in range(2 * chips)])

    def late(place):
        return int(place >= chips // 2)

    block = packed(clusters, embed, owner.reshape(1, rows), near)
    behind, ahead = [block], [block]
    for hop in range(1, hops + 1):
        behind.append(along(behind[-1], 1))
        ahead.append(along(ahead[-1], -1, late if hop == hops else lambda place: 0))
    spare = [other_core(half) for half in behind[:hops]]

    total = own_terms(clusters, block, spare[0])
    inner, sums = [block, spare[0]], None
    for hop in range(1, hops + 1):
        outer = [behind[hop]] if hop == hops else [behind[hop], spare[hop]]
        a_sums, b_sums = pair_sums(clusters, inner + outer, ahead[hop])
        if sums is not None:
            a_sums[0], a_sums[1] = a_sums[0] + sums[0], a_sums[1] + sums[1]
        done = a_sums[0] + other_core(a_sums[1])
        total = total + (done if hop == 1 else along(done, 1 - hop))
        if hop < hops:
            total = total + along(b_sums, hop)
            inner, sums = outer, a_sums[2:]
            continue
        route = []
        for place in range(chips):
            there = (place + hop) % chips
            for core in range(2):
                route.append((2 * order[place] + core, 2 * order[there] + (core ^ late(place))))
        total = total + lax.ppermute(b_sums, "blk", route)
        total = total + along(a_sums[2], -hop)
    return jnp.log1p(total)[0]


def solution(mesh):
    return jax.shard_map(
        per_device,
        mesh=mesh,
        in_specs=(P(("groups", "blk"), None), P(("groups", "blk"), None), P("groups")),
        out_specs=P(("groups", "blk")),
        check_vma=False,
    )
```

```python
import functools

import jax
import jax.numpy as jnp
from jax import lax
from jax.experimental import pallas as pl
from jax.experimental.pallas import tpu as pltpu
from jax.sharding import PartitionSpec as P

STRIP = 256


def unit_rows(values):
    values = values.astype(jnp.float32)
    width = values.shape[-1]
    scale = lax.rsqrt(jnp.mean(values * values, axis=-1, keepdims=True) + 1e-06) / jnp.sqrt(
        jnp.float32(width)
    )
    return (values * scale).astype(jnp.bfloat16)


def as_column(row):
    return jnp.transpose(jnp.broadcast_to(row, (128, row.shape[1])))


def nearest(own, near, clusters):
    step = jnp.zeros_like(own)
    for name in range(clusters):
        step = jnp.where(own == name, 2 * near[name] - 1, step)
    other = own + step
    other = jnp.where(other < 0, other + clusters, other)
    return jnp.where(other >= clusters, other - clusters, other)


def terms(a_unit, b_unit, a_own, a_near, b_own, b_near):
    sim = lax.dot_general(
        a_unit, b_unit, (((1,), (1,)), ((), ())), preferred_element_type=jnp.float32
    )
    wide = sim.shape[1] // 128
    a_own, a_near = jnp.tile(a_own, (1, wide)), jnp.tile(a_near, (1, wide))
    near = jnp.where(a_near == b_own, 0.5, 0.0) + jnp.where(a_own == b_near, 0.5, 0.0)
    return jnp.where(a_own == b_own, 1.0, near) * jnp.exp(16.0 * sim)


def lanes_added(x):
    out = x[:, :128]
    for at in range(128, x.shape[1], 128):
        out = out + x[:, at : at + 128]
    return out


def as_row(x):
    return jnp.sum(jnp.transpose(x), axis=0, keepdims=True)


def normalise(source, target):
    for at in range(0, source.shape[0], STRIP):
        target[at : at + STRIP, :] = unit_rows(source[at : at + STRIP, :])


def codes(names, half, near, clusters):
    own = names[half : half + 1, :]
    return own, nearest(own, near, clusters)


def own_kernel(clusters, near, mine, other, names, mine_unit, other_unit, sums):
    normalise(mine, mine_unit)
    normalise(other, other_unit)
    a_own, a_near = [as_column(row) for row in codes(names, 0, near, clusters)]
    halves = [(unit, *codes(names, i, near, clusters)) for i, unit in enumerate((mine_unit, other_unit))]
    for at in range(0, mine.shape[0], STRIP):
        here = slice(at, at + STRIP)
        total = jnp.zeros((STRIP, 128), jnp.float32)
        for unit, b_own, b_near in halves:
            value = terms(mine_unit[here, :], unit[...], a_own[here], a_near[here], b_own, b_near)
            if unit is mine_unit:
                place = lax.broadcasted_iota(jnp.int32, value.shape, 0) + at
                same = place == lax.broadcasted_iota(jnp.int32, value.shape, 1)
                value = jnp.where(same, 0.0, value)
            total = total + lanes_added(value)
        sums[:, here] = as_row(total)


def pair_kernel(clusters, ready, raw, near, *refs):
    blocks = ready + raw
    a_rows, refs = refs[:blocks], refs[blocks:]
    inner, outer, b_rows, b_names, a_from = refs[:5]
    a_units = refs[5:-3]
    a_sums, b_sums, b_unit = refs[-3:]
    normalise(b_rows, b_unit)
    b_own, b_near = codes(b_names, 0, near, clusters)
    rows = b_rows.shape[0]
    b_total = jnp.zeros((8, rows), jnp.float32)
    for block in range(blocks):
        names, half = (inner, block) if block < ready else (outer, block - ready)
        a_own, a_near = [as_column(row) for row in codes(names, half, near, clusters)]
        unit = a_rows[block]
        if block >= ready:
            unit = a_units[block - ready]
            normalise(a_rows[block], unit)
        for at in range(0, rows, STRIP):
            here = slice(at, at + STRIP)
            value = terms(unit[here, :], b_unit[...], a_own[here], a_near[here], b_own, b_near)
            added = as_row(lanes_added(value))
            if block < a_from.shape[0]:
                added = added + a_from[block : block + 1, here]
            a_sums[block : block + 1, here] = added
            b_total = b_total + jnp.sum(value.reshape(STRIP // 8, 8, rows), axis=0)
    b_sums[...] = jnp.sum(b_total, axis=0, keepdims=True)


def vmem(count):
    return [pl.BlockSpec(memory_space=pltpu.VMEM)] * count


SMEM = pl.BlockSpec(memory_space=pltpu.SMEM)
PARAMS = pltpu.CompilerParams(vmem_limit_bytes=40 << 20)


def cost(tiles, rows, width):
    return pl.CostEstimate(
        flops=2 * tiles * rows * rows * width,
        bytes_accessed=4 * rows * width,
        transcendentals=tiles * rows * rows,
    )


def own_terms(near, mine, other, names):
    rows, width = mine.shape
    unit = jax.ShapeDtypeStruct((rows, width), jnp.bfloat16)
    return pl.pallas_call(
        functools.partial(own_kernel, near.shape[0]),
        out_shape=(unit, unit, jax.ShapeDtypeStruct((1, rows), jnp.float32)),
        in_specs=[SMEM] + vmem(3),
        out_specs=vmem(3),
        compiler_params=PARAMS,
        cost_estimate=cost(2, rows, width),
        name="own_terms",
    )(near, mine, other, names)


def pair_sums(near, ready, raw, inner, outer, b_rows, b_names, a_from):
    rows, width = b_rows.shape
    blocks = len(ready) + len(raw)
    unit = jax.ShapeDtypeStruct((rows, width), jnp.bfloat16)
    outs = pl.pallas_call(
        functools.partial(pair_kernel, near.shape[0], len(ready), len(raw)),
        out_shape=(unit,) * len(raw)
        + (
            jax.ShapeDtypeStruct((blocks, rows), jnp.float32),
            jax.ShapeDtypeStruct((1, rows), jnp.float32),
        ),
        in_specs=[SMEM] + vmem(blocks + 5),
        out_specs=vmem(len(raw) + 2),
        scratch_shapes=[pltpu.VMEM((rows, width), jnp.bfloat16)],
        compiler_params=PARAMS,
        cost_estimate=cost(blocks, rows, width),
        name="pair_sums",
    )(near, *ready, *raw, inner, outer, b_rows, b_names, a_from)
    return outs[: len(raw)], outs[-2], outs[-1]


def per_device(embed, owner, near):
    rows = embed.shape[0]
    chips = lax.axis_size("blk") // 2
    hops = chips // 4
    order = list(range(0, chips, 2)) + list(range(chips - 1, 0, -2))

    def sent(block, distance, crossed=lambda place: 0):
        route = []
        for place in range(chips):
            there = order[(place + distance) % chips]
            for core in range(2):
                route.append((2 * order[place] + core, 2 * there + (core ^ crossed(place))))
        return lax.ppermute(block, "blk", route)

    def other_core(block):
        return sent(block, 0, lambda place: 1)

    def late(place):
        return int(place % chips >= chips // 2)

    name = owner.reshape(1, rows)
    names = jnp.concatenate([name, other_core(name)], axis=0)
    behind, ahead, behind_names, ahead_names = [embed], [embed], [names], [names]
    for hop in range(1, hops + 1):
        if hop == 2:
            behind[1], ahead[1], behind_names[1], ahead_names[1] = lax.optimization_barrier(
                (behind[1], ahead[1], behind_names[1], ahead_names[1])
            )
        crossed = (lambda place: late(place - 1)) if hop == hops else (lambda place: 0)
        behind.append(sent(behind[-1], 1))
        ahead.append(sent(ahead[-1], -1, crossed))
        behind_names.append(sent(behind_names[-1], 1))
        ahead_names.append(sent(ahead_names[-1], -1, crossed))
    spare = [other_core(half) for half in behind[:hops]]

    unit, spare_unit, sums = own_terms(near, embed, spare[0], names)
    units, total = [unit, spare_unit], None
    for hop in range(1, hops + 1):
        last = hop == hops
        raw = [behind[hop]] if last else [behind[hop], spare[hop]]
        block = ahead[hop]
        if last and total is not None:
            block, total = lax.optimization_barrier((block, total))
        units, a_sums, b_sums = pair_sums(
            near, units, raw, behind_names[hop - 1], behind_names[hop], block, ahead_names[hop], sums
        )
        done = a_sums[0:1] + other_core(a_sums[1:2])
        total = done if hop == 1 else total + sent(done, 1 - hop)
        total = total + sent(b_sums, hop, late if last else (lambda place: 0))
        if last:
            total = total + sent(a_sums[2:3], -hop)
        sums = a_sums[2:]
    return jnp.log1p(total)[0]


def solution(mesh):
    return jax.shard_map(
        per_device,
        mesh=mesh,
        in_specs=(P(("groups", "blk"), None), P(("groups", "blk"), None), P("groups")),
        out_specs=P(("groups", "blk")),
        check_vma=False,
    )
```

```python
import functools

import jax
import jax.numpy as jnp
from jax import lax
from jax.experimental import pallas as pl
from jax.experimental.pallas import tpu as pltpu
from jax.sharding import PartitionSpec as P

STRIP = 256
SPLIT = 2
ROOM = 8


def unit_rows(values):
    values = values.astype(jnp.float32)
    width = values.shape[-1]
    scale = lax.rsqrt(jnp.mean(values * values, axis=-1, keepdims=True) + 1e-06) / jnp.sqrt(
        jnp.float32(width)
    )
    return (values * scale).astype(jnp.bfloat16)


def strips(rows):
    return [slice(at, min(at + STRIP, rows)) for at in range(0, rows, STRIP)]


def normalise(sources, target, raw=True):
    put = 0
    for source in sources:
        for here in strips(source.shape[0]):
            values = source[here, :]
            target[put + here.start : put + here.stop, :] = unit_rows(values) if raw else values
        put += source.shape[0]


def nearest(own, near, clusters):
    step = jnp.zeros_like(own)
    for name in range(clusters):
        step = jnp.where(own == name, 2 * near[name] - 1, step)
    other = own + step
    other = jnp.where(other < 0, other + clusters, other)
    return jnp.where(other >= clusters, other - clusters, other)


def as_column(row):
    return jnp.transpose(jnp.broadcast_to(row, (128, row.shape[1])))


def terms(a_unit, b_unit, a_own, a_near, b_own, b_near):
    sim = lax.dot_general(
        a_unit, b_unit, (((1,), (1,)), ((), ())), preferred_element_type=jnp.float32
    )
    wide = sim.shape[1] // 128
    a_own, a_near = jnp.tile(a_own, (1, wide)), jnp.tile(a_near, (1, wide))
    near = jnp.where(a_near == b_own, 0.5, 0.0) + jnp.where(a_own == b_near, 0.5, 0.0)
    return jnp.where(a_own == b_own, 1.0, near) * jnp.exp(16.0 * sim)


def lanes_added(x):
    out = x[:, :128]
    for at in range(128, x.shape[1], 128):
        out = out + x[:, at : at + 128]
    return out


def as_row(x):
    return jnp.sum(jnp.transpose(x), axis=0, keepdims=True)


def sums_kernel(clusters, blocks, lists, tasks, kept, near, *refs):
    units = []
    for pieces, *_ in blocks:
        units.append(refs[:pieces])
        refs = refs[pieces:]
    names, refs = refs[:lists], refs[lists:]
    before, sums, refs = (refs[0], refs[1], refs[2:]) if kept is None else (None, refs[0], refs[1:])
    kept = kept or ()
    given, scratch = refs[: len(kept)], list(refs[len(kept) :])
    codes = {}

    def code(block):
        if block not in codes:
            *_, at, row, place = blocks[block]
            own = names[at][row : row + 1, place : place + units[block].shape[0]]
            codes[block] = own, nearest(own, near, clusters)
        return codes[block]

    for block, (pieces, raw, *_) in enumerate(blocks):
        if raw or pieces > 1:
            target = given[kept.index(block)] if block in kept else scratch.pop(0)
            normalise(units[block], target, raw)
            units[block] = target
        else:
            (units[block],) = units[block]
    sums[...] = jnp.zeros_like(sums) if before is None else before[...]
    for task, (block, others) in enumerate(tasks):
        a_own, a_near = [as_column(row) for row in code(block)]
        place = blocks[block][-1]
        for here in strips(units[block].shape[0]):
            total = jnp.zeros((here.stop - here.start, 128), jnp.float32)
            for other in others:
                value = terms(
                    units[block][here, :], units[other][...], a_own[here], a_near[here], *code(other)
                )
                if other == block:
                    row = lax.broadcasted_iota(jnp.int32, value.shape, 0) + here.start
                    same = row == lax.broadcasted_iota(jnp.int32, value.shape, 1)
                    value = jnp.where(same, 0.0, value)
                total = total + lanes_added(value)
            sums[task : task + 1, place + here.start : place + here.stop] = as_row(total)


def row_sums(near, blocks, names, tasks, label, kept=(), before=None, room=0):
    blocks = [(block if isinstance(block, list) else [block], *rest) for block, *rest in blocks]
    width = blocks[0][0][0].shape[1]
    units = [
        jax.ShapeDtypeStruct((sum(piece.shape[0] for piece in block[0]), width), jnp.bfloat16)
        for block in blocks
    ]
    made = [i for i, block in enumerate(blocks) if block[1] or len(block[0]) > 1]
    scratch = [i for i in made if i not in kept]
    vmem = pl.BlockSpec(memory_space=pltpu.VMEM)
    operands = [piece for block in blocks for piece in block[0]] + names
    operands += [] if before is None else [before]
    sums, *given = pl.pallas_call(
        functools.partial(
            sums_kernel,
            near.shape[0],
            [(len(block[0]), *block[1:]) for block in blocks],
            len(names),
            tasks,
            kept if before is None else None,
        ),
        out_shape=[
            jax.ShapeDtypeStruct((max(len(tasks), room), names[0].shape[1]), jnp.float32),
            *[units[i] for i in kept],
        ],
        in_specs=[pl.BlockSpec(memory_space=pltpu.SMEM)] + [vmem] * len(operands),
        out_specs=[vmem] * (1 + len(kept)),
        scratch_shapes=[pltpu.VMEM(units[i].shape, jnp.bfloat16) for i in scratch],
        compiler_params=pltpu.CompilerParams(vmem_limit_bytes=40 << 20),
        cost_estimate=pl.CostEstimate(flops=0, bytes_accessed=0, transcendentals=0),
        name=label,
    )(near, *operands)
    return sums, given


def unit_block(rows):
    vmem = pl.BlockSpec(memory_space=pltpu.VMEM)
    return pl.pallas_call(
        lambda source, target: normalise([source], target),
        out_shape=jax.ShapeDtypeStruct(rows.shape, jnp.bfloat16),
        in_specs=[vmem],
        out_specs=vmem,
        compiler_params=pltpu.CompilerParams(vmem_limit_bytes=40 << 20),
        cost_estimate=pl.CostEstimate(flops=0, bytes_accessed=0, transcendentals=0),
        name="unit_rows",
    )(rows)


def per_device(embed, owner, near):
    rows = embed.shape[0]
    chips = lax.axis_size("blk") // 2
    hops = chips // 4
    order = list(range(0, chips, 2)) + list(range(chips - 1, 0, -2))

    def moved(block, target):
        route = []
        for place in range(chips):
            for core in range(2):
                there, to = target(place, core)
                route.append((2 * order[place] + core, 2 * order[there % chips] + to))
        return lax.ppermute(block, "blk", route)

    def other_core(block):
        return moved(block, lambda place, core: (place, 1 - core))

    def late(place):
        return int(place % chips >= chips // 2)

    def onward(distance):
        return lambda place, core: (place + distance * (1 - 2 * core), core)

    def first(half):
        def target(place, core):
            forward = core == late(place + hops) ^ half
            return (place + 1, 0) if forward else (place - 1, 1)

        return target

    def back(distance, half):
        def target(place, core):
            home = place - distance * (1 - 2 * core)
            return home, late(home + hops * (1 - 2 * core)) ^ half

        return target

    name = owner.reshape(1, rows)
    own_names = jnp.concatenate([name, other_core(name)], axis=0)
    swapped = lax.axis_index("blk") // 2 >= chips // 2
    sent_names = jnp.where(swapped, own_names[::-1], own_names)
    side_names = [own_names] + [moved(sent_names, onward(h)) for h in range(1, hops + 1)]
    side = [None, [moved(embed, first(half)) for half in range(2)]]
    total, own = row_sums(
        near,
        [(embed, True, 0, 0, 0), (other_core(embed), True, 0, 1, 0)],
        [own_names],
        ((0, (0, 1)),),
        "own_terms",
        (0,),
    )
    if hops > 1:
        side[1][0], total, side_names[1] = lax.optimization_barrier((side[1][0], total, side_names[1]))
    side[1][1] = unit_block(side[1][1])
    for hop in range(2, hops + 1):
        side.append([moved(half, onward(1)) for half in side[-1]])
    *ready, side_names = lax.optimization_barrier((*side[1], side_names))
    across = [None] + [
        [[other_core(part) for part in jnp.split(half, SPLIT)] for half in pair]
        for pair in [ready, *side[2:hops]]
    ]
    across_names = [other_core(pair) for pair in side_names]

    inner = None
    for hop in range(1, hops):
        blocks = [(half, i == 0, 0, i, 0) for i, half in enumerate(side[hop])]
        blocks += [(half, i == 0, 1, i, 0) for i, half in enumerate(across[hop])]
        if hop == 1:
            blocks += [(own[0], False, 2, 0, 0)]
            names = [side_names[1], across_names[1], own_names]
            tasks = ((0, (2, 3)), (1, (2, 3)), (4, (0, 1, 2, 3)))
        else:
            blocks += [(half, False, 2, i, 0) for i, half in enumerate(inner)]
            names = [side_names[hop], across_names[hop], across_names[hop - 1]]
            tasks = ((0, (2, 3, 4, 5)), (1, (2, 3, 4, 5)))
        sums, inner = row_sums(near, blocks, names, tasks, "pair_terms", (2, 3))
        for half in range(2):
            total = total + moved(sums[half : half + 1], back(hop, half))
        if hop == 1:
            total = total + sums[2:]
    facing, *inner = lax.optimization_barrier((side[hops][0], *inner))
    facing = [other_core(part) for part in jnp.split(facing, SPLIT)]
    names = [side_names[hops], across_names[hops], across_names[hops - 1]]
    others = [(unit, False, 2, i, 0) for i, unit in enumerate(inner)]
    task = ((0, (1, 2, 3)),)
    blocks = [(side[hops][0], True, 0, 0, 0), (facing, True, 1, 0, 0), *others]
    sums, (facing,) = row_sums(near, blocks, names, task, "end_terms", (1,), room=ROOM)
    total = total + moved(sums, back(hops, 0))[:1]
    others = [(facing, False, 1, 0, 0), *others]
    sums, _ = row_sums(near, [(side[hops][1], False, 0, 1, 0), *others], names, task, "end_terms")
    total = total + moved(sums, back(hops, 1))
    return jnp.log1p(total)[0]


def solution(mesh):
    return jax.shard_map(
        per_device,
        mesh=mesh,
        in_specs=(P(("groups", "blk"), None), P(("groups", "blk"), None), P("groups")),
        out_specs=P(("groups", "blk")),
        check_vma=False,
    )
```

```python
import functools

import jax
import jax.numpy as jnp
from jax import lax
from jax.experimental import pallas as pl
from jax.experimental.pallas import tpu as pltpu
from jax.sharding import PartitionSpec as P

STRIP = 256
SPLIT = 2
ROOM = 8


def unit_rows(values):
    values = values.astype(jnp.float32)
    width = values.shape[-1]
    scale = lax.rsqrt(jnp.mean(values * values, axis=-1, keepdims=True) + 1e-06) / jnp.sqrt(
        jnp.float32(width)
    )
    return (values * scale).astype(jnp.bfloat16)


def strips(rows):
    return [slice(at, min(at + STRIP, rows)) for at in range(0, rows, STRIP)]


def normalise(sources, target, raw=True):
    put = 0
    for source in sources:
        for here in strips(source.shape[0]):
            values = source[here, :]
            target[put + here.start : put + here.stop, :] = unit_rows(values) if raw else values
        put += source.shape[0]


def nearest(own, near, clusters):
    step = jnp.zeros_like(own)
    for name in range(clusters):
        step = jnp.where(own == name, 2 * near[name] - 1, step)
    other = own + step
    other = jnp.where(other < 0, other + clusters, other)
    return jnp.where(other >= clusters, other - clusters, other)


def as_column(row):
    return jnp.transpose(jnp.broadcast_to(row, (128, row.shape[1])))


def terms(a_unit, b_unit, a_own, a_near, b_own, b_near):
    sim = lax.dot_general(
        a_unit, b_unit, (((1,), (1,)), ((), ())), preferred_element_type=jnp.float32
    )
    wide = sim.shape[1] // 128
    a_own, a_near = jnp.tile(a_own, (1, wide)), jnp.tile(a_near, (1, wide))
    near = jnp.where(a_near == b_own, 0.5, 0.0) + jnp.where(a_own == b_near, 0.5, 0.0)
    return jnp.where(a_own == b_own, 1.0, near) * jnp.exp(16.0 * sim)


def lanes_added(x):
    out = x[:, :128]
    for at in range(128, x.shape[1], 128):
        out = out + x[:, at : at + 128]
    return out


def as_row(x):
    return jnp.sum(jnp.transpose(x), axis=0, keepdims=True)


def sums_kernel(clusters, blocks, lists, tasks, kept, near, *refs):
    units = []
    for pieces, *_ in blocks:
        units.append(refs[:pieces])
        refs = refs[pieces:]
    names, refs = refs[:lists], refs[lists:]
    before, sums, refs = (refs[0], refs[1], refs[2:]) if kept is None else (None, refs[0], refs[1:])
    kept = kept or ()
    given, scratch = refs[: len(kept)], list(refs[len(kept) :])
    codes = {}

    def code(block):
        if block not in codes:
            *_, at, row, place = blocks[block]
            own = names[at][row : row + 1, place : place + units[block].shape[0]]
            codes[block] = own, nearest(own, near, clusters)
        return codes[block]

    for block, (pieces, raw, *_) in enumerate(blocks):
        if raw or pieces > 1:
            target = given[kept.index(block)] if block in kept else scratch.pop(0)
            normalise(units[block], target, raw)
            units[block] = target
        else:
            (units[block],) = units[block]
    sums[...] = jnp.zeros_like(sums) if before is None else before[...]
    for task, (block, others) in enumerate(tasks):
        a_own, a_near = [as_column(row) for row in code(block)]
        place = blocks[block][-1]
        for here in strips(units[block].shape[0]):
            total = jnp.zeros((here.stop - here.start, 128), jnp.float32)
            for other in others:
                value = terms(
                    units[block][here, :], units[other][...], a_own[here], a_near[here], *code(other)
                )
                if other == block:
                    row = lax.broadcasted_iota(jnp.int32, value.shape, 0) + here.start
                    same = row == lax.broadcasted_iota(jnp.int32, value.shape, 1)
                    value = jnp.where(same, 0.0, value)
                total = total + lanes_added(value)
            sums[task : task + 1, place + here.start : place + here.stop] = as_row(total)


def row_sums(near, blocks, names, tasks, label, kept=(), before=None, room=0):
    blocks = [(block if isinstance(block, list) else [block], *rest) for block, *rest in blocks]
    width = blocks[0][0][0].shape[1]
    units = [
        jax.ShapeDtypeStruct((sum(piece.shape[0] for piece in block[0]), width), jnp.bfloat16)
        for block in blocks
    ]
    made = [i for i, block in enumerate(blocks) if block[1] or len(block[0]) > 1]
    scratch = [i for i in made if i not in kept]
    vmem = pl.BlockSpec(memory_space=pltpu.VMEM)
    operands = [piece for block in blocks for piece in block[0]] + names
    operands += [] if before is None else [before]
    sums, *given = pl.pallas_call(
        functools.partial(
            sums_kernel,
            near.shape[0],
            [(len(block[0]), *block[1:]) for block in blocks],
            len(names),
            tasks,
            kept if before is None else None,
        ),
        out_shape=[
            jax.ShapeDtypeStruct((max(len(tasks), room), names[0].shape[1]), jnp.float32),
            *[units[i] for i in kept],
        ],
        in_specs=[pl.BlockSpec(memory_space=pltpu.SMEM)] + [vmem] * len(operands),
        out_specs=[vmem] * (1 + len(kept)),
        scratch_shapes=[pltpu.VMEM(units[i].shape, jnp.bfloat16) for i in scratch],
        compiler_params=pltpu.CompilerParams(vmem_limit_bytes=40 << 20),
        cost_estimate=pl.CostEstimate(flops=0, bytes_accessed=0, transcendentals=0),
        name=label,
    )(near, *operands)
    return sums, given


def unit_block(rows):
    vmem = pl.BlockSpec(memory_space=pltpu.VMEM)
    return pl.pallas_call(
        lambda source, target: normalise([source], target),
        out_shape=jax.ShapeDtypeStruct(rows.shape, jnp.bfloat16),
        in_specs=[vmem],
        out_specs=vmem,
        compiler_params=pltpu.CompilerParams(vmem_limit_bytes=40 << 20),
        cost_estimate=pl.CostEstimate(flops=0, bytes_accessed=0, transcendentals=0),
        name="unit_rows",
    )(rows)


def per_device(embed, owner, near):
    rows = embed.shape[0]
    chips = lax.axis_size("blk") // 2
    hops = chips // 4
    order = list(range(0, chips, 2)) + list(range(chips - 1, 0, -2))

    def moved(block, target):
        route = []
        for place in range(chips):
            for core in range(2):
                there, to = target(place, core)
                route.append((2 * order[place] + core, 2 * order[there % chips] + to))
        return lax.ppermute(block, "blk", route)

    def other_core(block):
        return moved(block, lambda place, core: (place, 1 - core))

    def onward(place, core):
        return place + 1 - 2 * core, core

    def against(place, core):
        return place - 1 + 2 * core, 1 - core

    def back(distance, half):
        return lambda place, core: (place - distance * (1 - 2 * core), core ^ half)

    name = owner.reshape(1, rows)
    other_name, other = other_core(name), other_core(embed)
    own_names = jnp.concatenate([name, other_name], axis=0)
    side_names, across_names = [own_names], [jnp.concatenate([other_name, name], axis=0)]
    for hop in range(1, hops + 1):
        side_names.append(moved(across_names[-1], against))
        across_names.append(other_core(side_names[-1]))
    total, own = row_sums(
        near,
        [(embed, True, 0, 0, 0), (other, True, 0, 1, 0)],
        [own_names],
        ((0, (0, 1)),),
        "own_terms",
        (0,),
    )
    first, second = moved(embed, onward), moved(other, onward)
    first, total, side_names, across_names = lax.optimization_barrier(
        (first, total, side_names, across_names)
    )
    side = [None, [first, unit_block(second)]]
    for hop in range(2, hops + 1):
        side.append([moved(half, onward) for half in side[-1]])
    across = [None] + [
        [[other_core(part) for part in jnp.split(half, SPLIT)] for half in pair]
        for pair in side[1:hops]
    ]

    inner = None
    for hop in range(1, hops):
        blocks = [(half, i == 0, 0, i, 0) for i, half in enumerate(side[hop])]
        blocks += [(half, i == 0, 1, i, 0) for i, half in enumerate(across[hop])]
        if hop == 1:
            blocks += [(own[0], False, 2, 0, 0)]
            names = [side_names[1], across_names[1], own_names]
            tasks = ((0, (2, 3)), (1, (2, 3)), (4, (0, 1, 2, 3)))
        else:
            blocks += [(half, False, 2, i, 0) for i, half in enumerate(inner)]
            names = [side_names[hop], across_names[hop], across_names[hop - 1]]
            tasks = ((0, (2, 3, 4, 5)), (1, (2, 3, 4, 5)))
        sums, inner = row_sums(near, blocks, names, tasks, "pair_terms", (2, 3))
        for half in range(2):
            total = total + moved(sums[half : half + 1], back(hop, half))
        if hop == 1:
            total = total + sums[2:]
    facing, *inner = lax.optimization_barrier((side[hops][0], *inner))
    facing = [other_core(part) for part in jnp.split(facing, SPLIT)]
    names = [side_names[hops], across_names[hops], across_names[hops - 1]]
    others = [(unit, False, 2, i, 0) for i, unit in enumerate(inner)]
    task = ((0, (1, 2, 3)),)
    blocks = [(side[hops][0], True, 0, 0, 0), (facing, True, 1, 0, 0), *others]
    sums, (facing,) = row_sums(near, blocks, names, task, "end_terms", (1,), room=ROOM)
    total = total + moved(sums, back(hops, 0))[:1]
    others = [(facing, False, 1, 0, 0), *others]
    sums, _ = row_sums(near, [(side[hops][1], False, 0, 1, 0), *others], names, task, "end_terms")
    total = total + moved(sums, back(hops, 1))
    return jnp.log1p(total)[0]


def solution(mesh):
    return jax.shard_map(
        per_device,
        mesh=mesh,
        in_specs=(P(("groups", "blk"), None), P(("groups", "blk"), None), P("groups")),
        out_specs=P(("groups", "blk")),
        check_vma=False,
    )
```

```python
import functools

import jax
import jax.numpy as jnp
from jax import lax
from jax.experimental import pallas as pl
from jax.experimental.pallas import tpu as pltpu
from jax.sharding import PartitionSpec as P

STRIP = 256
SPLIT = 2
ROOM = 8
END_ROOM = 4


def unit_rows(values):
    values = values.astype(jnp.float32)
    width = values.shape[-1]
    scale = lax.rsqrt(jnp.mean(values * values, axis=-1, keepdims=True) + 1e-06) / jnp.sqrt(
        jnp.float32(width)
    )
    return (values * scale).astype(jnp.bfloat16)


def strips(rows):
    return [slice(at, min(at + STRIP, rows)) for at in range(0, rows, STRIP)]


def normalise(sources, target, raw=True):
    put = 0
    for source in sources:
        for here in strips(source.shape[0]):
            values = source[here, :]
            target[put + here.start : put + here.stop, :] = unit_rows(values) if raw else values
        put += source.shape[0]


def nearest(own, near, clusters):
    step = jnp.zeros_like(own)
    for name in range(clusters):
        step = jnp.where(own == name, 2 * near[name] - 1, step)
    other = own + step
    other = jnp.where(other < 0, other + clusters, other)
    return jnp.where(other >= clusters, other - clusters, other)


def as_column(row):
    return jnp.transpose(jnp.broadcast_to(row, (128, row.shape[1])))


def terms(a_unit, b_unit, a_own, a_near, b_own, b_near):
    sim = lax.dot_general(
        a_unit, b_unit, (((1,), (1,)), ((), ())), preferred_element_type=jnp.float32
    )
    wide = sim.shape[1] // 128
    a_own, a_near = jnp.tile(a_own, (1, wide)), jnp.tile(a_near, (1, wide))
    near = jnp.where(a_near == b_own, 0.5, 0.0) + jnp.where(a_own == b_near, 0.5, 0.0)
    return jnp.where(a_own == b_own, 1.0, near) * jnp.exp(16.0 * sim)


def lanes_added(x):
    out = x[:, :128]
    for at in range(128, x.shape[1], 128):
        out = out + x[:, at : at + 128]
    return out


def as_row(x):
    return jnp.sum(jnp.transpose(x), axis=0, keepdims=True)


def sums_kernel(clusters, blocks, lists, tasks, kept, added, near, *refs):
    units = []
    for pieces, *_ in blocks:
        units.append(refs[:pieces])
        refs = refs[pieces:]
    names, refs = refs[:lists], refs[lists:]
    before, sums, refs = refs[:added], refs[added], refs[added + 1 :]
    given, scratch = refs[: len(kept)], list(refs[len(kept) :])
    codes = {}

    def code(block):
        if block not in codes:
            *_, at, row, place = blocks[block]
            own = names[at][row : row + 1, place : place + units[block].shape[0]]
            codes[block] = own, nearest(own, near, clusters)
        return codes[block]

    for block, (pieces, raw, *_) in enumerate(blocks):
        if raw or pieces > 1:
            target = given[kept.index(block)] if block in kept else scratch.pop(0)
            normalise(units[block], target, raw)
            units[block] = target
        else:
            (units[block],) = units[block]
    sums[...] = before[0][...] if added else jnp.zeros_like(sums)
    for task, block, others in tasks:
        a_own, a_near = [as_column(row) for row in code(block)]
        place = blocks[block][-1]
        for here in strips(units[block].shape[0]):
            total = jnp.zeros((here.stop - here.start, 128), jnp.float32)
            for other in others:
                value = terms(
                    units[block][here, :], units[other][...], a_own[here], a_near[here], *code(other)
                )
                if other == block:
                    row = lax.broadcasted_iota(jnp.int32, value.shape, 0) + here.start
                    same = row == lax.broadcasted_iota(jnp.int32, value.shape, 1)
                    value = jnp.where(same, 0.0, value)
                total = total + lanes_added(value)
            sums[task : task + 1, place + here.start : place + here.stop] += as_row(total)


def row_sums(near, blocks, names, tasks, label, kept=(), before=None, room=1):
    blocks = [(block if isinstance(block, list) else [block], *rest) for block, *rest in blocks]
    width = blocks[0][0][0].shape[1]
    units = [
        jax.ShapeDtypeStruct((sum(piece.shape[0] for piece in block[0]), width), jnp.bfloat16)
        for block in blocks
    ]
    made = [i for i, block in enumerate(blocks) if block[1] or len(block[0]) > 1]
    scratch = [i for i in made if i not in kept]
    vmem = pl.BlockSpec(memory_space=pltpu.VMEM)
    operands = [piece for block in blocks for piece in block[0]] + names
    operands += [] if before is None else [before]
    sums, *given = pl.pallas_call(
        functools.partial(
            sums_kernel,
            near.shape[0],
            [(len(block[0]), *block[1:]) for block in blocks],
            len(names),
            tasks,
            kept,
            int(before is not None),
        ),
        out_shape=[
            jax.ShapeDtypeStruct((room, names[0].shape[1]), jnp.float32),
            *[units[i] for i in kept],
        ],
        in_specs=[pl.BlockSpec(memory_space=pltpu.SMEM)] + [vmem] * len(operands),
        out_specs=[vmem] * (1 + len(kept)),
        scratch_shapes=[pltpu.VMEM(units[i].shape, jnp.bfloat16) for i in scratch],
        compiler_params=pltpu.CompilerParams(vmem_limit_bytes=40 << 20),
        cost_estimate=pl.CostEstimate(flops=0, bytes_accessed=0, transcendentals=0),
        name=label,
    )(near, *operands)
    return sums, given


def unit_block(rows):
    vmem = pl.BlockSpec(memory_space=pltpu.VMEM)
    return pl.pallas_call(
        lambda source, target: normalise([source], target),
        out_shape=jax.ShapeDtypeStruct(rows.shape, jnp.bfloat16),
        in_specs=[vmem],
        out_specs=vmem,
        compiler_params=pltpu.CompilerParams(vmem_limit_bytes=40 << 20),
        cost_estimate=pl.CostEstimate(flops=0, bytes_accessed=0, transcendentals=0),
        name="unit_rows",
    )(rows)


def per_device(embed, owner, near):
    rows = embed.shape[0]
    chips = lax.axis_size("blk") // 2
    hops = chips // 4
    order = list(range(0, chips, 2)) + list(range(chips - 1, 0, -2))

    def moved(block, target):
        route = []
        for place in range(chips):
            for core in range(2):
                there, to = target(place, core)
                route.append((2 * order[place] + core, 2 * order[there % chips] + to))
        return lax.ppermute(block, "blk", route)

    def other_core(block):
        return moved(block, lambda place, core: (place, 1 - core))

    def onward(place, core):
        return place + 1 - 2 * core, core

    def against(place, core):
        return place - 1 + 2 * core, 1 - core

    def back(distance, half=0):
        return lambda place, core: (place - distance * (1 - 2 * core), core ^ half)

    def split_swap(half):
        return [other_core(part) for part in jnp.split(half, SPLIT)]

    name = owner.reshape(1, rows)
    other_name, other = other_core(name), other_core(embed)
    own_names = jnp.concatenate([name, other_name], axis=0)
    side_names, across_names = [own_names], [jnp.concatenate([other_name, name], axis=0)]
    for hop in range(1, hops + 1):
        side_names.append(moved(across_names[-1], against))
        across_names.append(other_core(side_names[-1]))
    total, own = row_sums(
        near,
        [(embed, True, 0, 0, 0), (other, True, 0, 1, 0)],
        [own_names],
        ((0, 0, (0, 1)),),
        "own_terms",
        (0,),
    )
    first, second = moved(embed, onward), moved(other, onward)
    first, total, side_names, across_names = lax.optimization_barrier(
        (first, total, side_names, across_names)
    )
    swapped = [None, [split_swap(first)]]
    blocks = [(first, True, 0, 0, 0), (swapped[1][0], True, 1, 0, 0), (own[0], False, 2, 0, 0)]
    sums, units = row_sums(
        near,
        blocks,
        [side_names[1], across_names[1], own_names],
        ((0, 0, (1,)), (2, 2, (0, 1))),
        "first_terms",
        (0, 1),
        room=3,
    )
    second, sums = lax.optimization_barrier((second, sums))
    side = [None, [first, unit_block(second)]]
    for hop in range(2, hops + 1):
        halves = side[-1]
        side.append([moved(half, onward) for half in halves])
    across = [None, [swapped[1][0], split_swap(side[1][1])]]
    across += [[split_swap(half) for half in pair] for pair in side[2:hops]]

    inner, theirs = None, 0.0
    for hop in range(1, hops):
        blocks = [(side[hop][0], True, 0, 0, 0), (across[hop][0], True, 1, 0, 0)]
        if hop == 1:
            extra, names = [(own[0], False, 2, 0, 0)], [side_names[1], across_names[1], own_names]
            late = ((0, 0, (3,)), (1, 2, (1, 3)), (2, 4, (2, 3)))
        else:
            extra = [(unit, False, 2, i, 0) for i, unit in enumerate(inner)]
            names = [side_names[hop], across_names[hop], across_names[hop - 1]]
            early = ((0, 0, (1, 2, 3)),)
            late = ((0, 0, (3,)), (1, 2, (1, 3, 4, 5)))
        if hop > 1:
            sums, units = row_sums(
                near, [*blocks, *extra], names, early, "first_terms", (0, 1), room=3
            )
        blocks = [(unit, False, i, 0, 0) for i, unit in enumerate(units)]
        blocks += [(side[hop][1], False, 0, 1, 0), (across[hop][1], False, 1, 1, 0), *extra]
        sums, (unit,) = row_sums(near, blocks, names, late, "pair_terms", (3,), before=sums, room=3)
        inner = [units[1], unit]
        returned = moved(sums[:2], back(hop))
        if hop == 1:
            total = total + sums[2:3]
        if hop < hops - 1:
            total, theirs = total + returned[:1], theirs + returned[1:]
    facing, returned, *inner = lax.optimization_barrier((side[hops][0], returned, *inner))
    facing = split_swap(facing)
    total = total + returned[:1] + other_core(theirs + returned[1:])
    names = [side_names[hops], across_names[hops], across_names[hops - 1]]
    blocks = [(side[hops][0], True, 0, 0, 0)]
    blocks += [(unit, False, 2, i, 0) for i, unit in enumerate(inner)]
    tasks = ((0, 0, (2,)), (1, 1, (0,)), (2, 2, (0,)))
    sums, (unit,) = row_sums(near, blocks, names, tasks, "end_terms", (0,), room=ROOM)
    for half in range(2):
        total = total + moved(sums, back(1 - hops, 1 - half))[1 + half : 2 + half]
    blocks = [(unit, False, 0, 0, 0), (facing, True, 1, 0, 0)]
    sums, (facing,) = row_sums(
        near, blocks, names, ((0, 0, (1,)),), "end_terms", (1,), before=sums[:END_ROOM], room=END_ROOM
    )
    total = total + moved(sums, back(hops))[:1]
    blocks = [(side[hops][1], False, 0, 1, 0), (facing, False, 1, 0, 0), (inner[1], False, 2, 1, 0)]
    sums, _ = row_sums(near, blocks, names, ((0, 0, (1, 2)),), "end_terms")
    total = total + moved(sums, back(hops, 1))
    return jnp.log1p(total)[0]


def solution(mesh):
    return jax.shard_map(
        per_device,
        mesh=mesh,
        in_specs=(P(("groups", "blk"), None), P(("groups", "blk"), None), P("groups")),
        out_specs=P(("groups", "blk")),
        check_vma=False,
    )
```

```python
import functools

import jax
import jax.numpy as jnp
from jax import lax
from jax.experimental import pallas as pl
from jax.experimental.pallas import tpu as pltpu
from jax.sharding import PartitionSpec as P

STRIP = 256
SPLIT = 2
ROOM = 8
END_ROOM = 4


def unit_rows(values):
    values = values.astype(jnp.float32)
    width = values.shape[-1]
    scale = lax.rsqrt(jnp.mean(values * values, axis=-1, keepdims=True) + 1e-06) / jnp.sqrt(
        jnp.float32(width)
    )
    return (values * scale).astype(jnp.bfloat16)


def strips(rows):
    return [slice(at, min(at + STRIP, rows)) for at in range(0, rows, STRIP)]


def normalise(sources, target, raw=True):
    put = 0
    for source in sources:
        for here in strips(source.shape[0]):
            values = source[here, :]
            target[put + here.start : put + here.stop, :] = unit_rows(values) if raw else values
        put += source.shape[0]


def nearest(own, near, clusters):
    step = jnp.zeros_like(own)
    for name in range(clusters):
        step = jnp.where(own == name, 2 * near[name] - 1, step)
    other = own + step
    other = jnp.where(other < 0, other + clusters, other)
    return jnp.where(other >= clusters, other - clusters, other)


def as_column(row):
    return jnp.transpose(jnp.broadcast_to(row, (128, row.shape[1])))


def terms(a_unit, b_unit, a_own, a_near, b_own, b_near):
    sim = lax.dot_general(
        a_unit, b_unit, (((1,), (1,)), ((), ())), preferred_element_type=jnp.float32
    )
    wide = sim.shape[1] // 128
    a_own, a_near = jnp.tile(a_own, (1, wide)), jnp.tile(a_near, (1, wide))
    near = jnp.where(a_near == b_own, 0.5, 0.0) + jnp.where(a_own == b_near, 0.5, 0.0)
    return jnp.where(a_own == b_own, 1.0, near) * jnp.exp(16.0 * sim)


def lanes_added(x):
    out = x[:, :128]
    for at in range(128, x.shape[1], 128):
        out = out + x[:, at : at + 128]
    return out


def as_row(x):
    return jnp.sum(jnp.transpose(x), axis=0, keepdims=True)


def sums_kernel(blocks, lists, tasks, kept, added, *refs):
    units = []
    for pieces, *_ in blocks:
        units.append(refs[:pieces])
        refs = refs[pieces:]
    names, refs = refs[:lists], refs[lists:]
    before, sums, refs = refs[:added], refs[added], refs[added + 1 :]
    given, scratch = refs[: len(kept)], list(refs[len(kept) :])
    codes = {}

    def code(block):
        if block not in codes:
            *_, at, row, place = blocks[block]
            here = slice(place, place + units[block].shape[0])
            codes[block] = names[at][row : row + 1, here], names[at][row + 2 : row + 3, here]
        return codes[block]

    for block, (pieces, raw, *_) in enumerate(blocks):
        if raw or pieces > 1:
            target = given[kept.index(block)] if block in kept else scratch.pop(0)
            normalise(units[block], target, raw)
            units[block] = target
        else:
            (units[block],) = units[block]
    sums[...] = before[0][...] if added else jnp.zeros_like(sums)
    for task, block, others in tasks:
        a_own, a_near = [as_column(row) for row in code(block)]
        place = blocks[block][-1]
        for here in strips(units[block].shape[0]):
            total = jnp.zeros((here.stop - here.start, 128), jnp.float32)
            for other in others:
                value = terms(
                    units[block][here, :], units[other][...], a_own[here], a_near[here], *code(other)
                )
                if other == block:
                    row = lax.broadcasted_iota(jnp.int32, value.shape, 0) + here.start
                    same = row == lax.broadcasted_iota(jnp.int32, value.shape, 1)
                    value = jnp.where(same, 0.0, value)
                total = total + lanes_added(value)
            sums[task : task + 1, place + here.start : place + here.stop] += as_row(total)


def row_sums(blocks, names, tasks, label, kept=(), before=None, room=1):
    blocks = [(block if isinstance(block, list) else [block], *rest) for block, *rest in blocks]
    width = blocks[0][0][0].shape[1]
    units = [
        jax.ShapeDtypeStruct((sum(piece.shape[0] for piece in block[0]), width), jnp.bfloat16)
        for block in blocks
    ]
    made = [i for i, block in enumerate(blocks) if block[1] or len(block[0]) > 1]
    scratch = [i for i in made if i not in kept]
    vmem = pl.BlockSpec(memory_space=pltpu.VMEM)
    operands = [piece for block in blocks for piece in block[0]] + names
    operands += [] if before is None else [before]
    sums, *given = pl.pallas_call(
        functools.partial(
            sums_kernel,
            [(len(block[0]), *block[1:]) for block in blocks],
            len(names),
            tasks,
            kept,
            int(before is not None),
        ),
        out_shape=[
            jax.ShapeDtypeStruct((room, names[0].shape[1]), jnp.float32),
            *[units[i] for i in kept],
        ],
        in_specs=[vmem] * len(operands),
        out_specs=[vmem] * (1 + len(kept)),
        scratch_shapes=[pltpu.VMEM(units[i].shape, jnp.bfloat16) for i in scratch],
        compiler_params=pltpu.CompilerParams(vmem_limit_bytes=40 << 20),
        cost_estimate=pl.CostEstimate(flops=0, bytes_accessed=0, transcendentals=0),
        name=label,
    )(*operands)
    return sums, given


def names_kernel(clusters, near, name, other, mine, swapped):
    both = [ref[...] for ref in (name, other)]
    both += [nearest(own, near, clusters) for own in both]
    for at, row in enumerate(both):
        mine[at : at + 1, :] = row
        swapped[at ^ 1 : (at ^ 1) + 1, :] = row


def name_tables(near, name, other):
    table = jax.ShapeDtypeStruct((4, name.shape[1]), jnp.int32)
    vmem = pl.BlockSpec(memory_space=pltpu.VMEM)
    return pl.pallas_call(
        functools.partial(names_kernel, near.shape[0]),
        out_shape=(table, table),
        in_specs=[pl.BlockSpec(memory_space=pltpu.SMEM), vmem, vmem],
        out_specs=(vmem, vmem),
        compiler_params=pltpu.CompilerParams(vmem_limit_bytes=40 << 20),
        cost_estimate=pl.CostEstimate(flops=0, bytes_accessed=0, transcendentals=0),
        name="name_tables",
    )(near, name, other)


def unit_block(rows):
    vmem = pl.BlockSpec(memory_space=pltpu.VMEM)
    return pl.pallas_call(
        lambda source, target: normalise([source], target),
        out_shape=jax.ShapeDtypeStruct(rows.shape, jnp.bfloat16),
        in_specs=[vmem],
        out_specs=vmem,
        compiler_params=pltpu.CompilerParams(vmem_limit_bytes=40 << 20),
        cost_estimate=pl.CostEstimate(flops=0, bytes_accessed=0, transcendentals=0),
        name="unit_rows",
    )(rows)


def per_device(embed, owner, near):
    rows = embed.shape[0]
    chips = lax.axis_size("blk") // 2
    hops = chips // 4
    order = list(range(0, chips, 2)) + list(range(chips - 1, 0, -2))

    def moved(block, target):
        route = []
        for place in range(chips):
            for core in range(2):
                there, to = target(place, core)
                route.append((2 * order[place] + core, 2 * order[there % chips] + to))
        return lax.ppermute(block, "blk", route)

    def other_core(block):
        return moved(block, lambda place, core: (place, 1 - core))

    def onward(place, core):
        return place + 1 - 2 * core, core

    def against(place, core):
        return place - 1 + 2 * core, 1 - core

    def back(distance, half=0):
        return lambda place, core: (place - distance * (1 - 2 * core), core ^ half)

    def split_swap(half):
        return [other_core(part) for part in jnp.split(half, SPLIT)]

    name = owner.reshape(1, rows)
    other_name, other = other_core(name), other_core(embed)
    own_names, swapped_names = name_tables(near, name, other_name)
    side_names, across_names = [own_names], [swapped_names]
    for hop in range(1, hops + 1):
        side_names.append(moved(across_names[-1], against))
        across_names.append(other_core(side_names[-1]))
    total, own = row_sums(
        [(embed, True, 0, 0, 0), (other, True, 0, 1, 0)],
        [own_names],
        ((0, 0, (0, 1)),),
        "own_terms",
        (0,),
    )
    first, second = moved(embed, onward), moved(other, onward)
    first, total, side_names, across_names = lax.optimization_barrier(
        (first, total, side_names, across_names)
    )
    swapped = [None, [split_swap(first)]]
    blocks = [(first, True, 0, 0, 0), (swapped[1][0], True, 1, 0, 0), (own[0], False, 2, 0, 0)]
    sums, units = row_sums(
        blocks,
        [side_names[1], across_names[1], own_names],
        ((0, 0, (1,)), (2, 2, (0, 1))),
        "first_terms",
        (0, 1),
        room=3,
    )
    second, sums = lax.optimization_barrier((second, sums))
    side = [None, [first, unit_block(second)]]
    for hop in range(2, hops + 1):
        halves = side[-1]
        side.append([moved(half, onward) for half in halves])
    across = [None, [swapped[1][0], split_swap(side[1][1])]]
    across += [[split_swap(half) for half in pair] for pair in side[2:hops]]

    inner, theirs = None, 0.0
    for hop in range(1, hops):
        blocks = [(side[hop][0], True, 0, 0, 0), (across[hop][0], True, 1, 0, 0)]
        if hop == 1:
            extra, names = [(own[0], False, 2, 0, 0)], [side_names[1], across_names[1], own_names]
            late = ((0, 0, (3,)), (1, 2, (1, 3)), (2, 4, (2, 3)))
        else:
            extra = [(unit, False, 2, i, 0) for i, unit in enumerate(inner)]
            names = [side_names[hop], across_names[hop], across_names[hop - 1]]
            early = ((0, 0, (1, 2, 3)),)
            late = ((0, 0, (3,)), (1, 2, (1, 3, 4, 5)))
        if hop > 1:
            sums, units = row_sums(
                [*blocks, *extra], names, early, "first_terms", (0, 1), room=3
            )
        blocks = [(unit, False, i, 0, 0) for i, unit in enumerate(units)]
        blocks += [(side[hop][1], False, 0, 1, 0), (across[hop][1], False, 1, 1, 0), *extra]
        sums, (unit,) = row_sums(blocks, names, late, "pair_terms", (3,), before=sums, room=3)
        inner = [units[1], unit]
        returned = moved(sums[:2], back(hop))
        if hop == 1:
            total = total + sums[2:3]
        if hop < hops - 1:
            total, theirs = total + returned[:1], theirs + returned[1:]
    facing, returned, *inner = lax.optimization_barrier((side[hops][0], returned, *inner))
    facing = split_swap(facing)
    total = total + returned[:1] + other_core(theirs + returned[1:])
    names = [side_names[hops], across_names[hops], across_names[hops - 1]]
    blocks = [(side[hops][0], True, 0, 0, 0)]
    blocks += [(unit, False, 2, i, 0) for i, unit in enumerate(inner)]
    tasks = ((0, 0, (2,)), (1, 1, (0,)), (2, 2, (0,)))
    sums, (unit,) = row_sums(blocks, names, tasks, "end_terms", (0,), room=ROOM)
    for half in range(2):
        total = total + moved(sums, back(1 - hops, 1 - half))[1 + half : 2 + half]
    blocks = [(unit, False, 0, 0, 0), (facing, True, 1, 0, 0)]
    sums, (facing,) = row_sums(
        blocks, names, ((0, 0, (1,)),), "end_terms", (1,), before=sums[:END_ROOM], room=END_ROOM
    )
    total = total + moved(sums, back(hops))[:1]
    blocks = [(side[hops][1], False, 0, 1, 0), (facing, False, 1, 0, 0), (inner[1], False, 2, 1, 0)]
    sums, _ = row_sums(blocks, names, ((0, 0, (1, 2)),), "end_terms")
    total = total + moved(sums, back(hops, 1))
    return jnp.log1p(total)[0]


def solution(mesh):
    return jax.shard_map(
        per_device,
        mesh=mesh,
        in_specs=(P(("groups", "blk"), None), P(("groups", "blk"), None), P("groups")),
        out_specs=P(("groups", "blk")),
        check_vma=False,
    )
```

```python
import functools

import jax
import jax.numpy as jnp
from jax import lax
from jax.experimental import pallas as pl
from jax.experimental.pallas import tpu as pltpu
from jax.sharding import PartitionSpec as P

STRIP = 256
SPLIT = 2
END_ROOM = 2


def unit_rows(values):
    values = values.astype(jnp.float32)
    width = values.shape[-1]
    scale = lax.rsqrt(jnp.mean(values * values, axis=-1, keepdims=True) + 1e-06) / jnp.sqrt(
        jnp.float32(width)
    )
    return (values * scale).astype(jnp.bfloat16)


def strips(rows):
    return [slice(at, min(at + STRIP, rows)) for at in range(0, rows, STRIP)]


def normalise(sources, target, raw=True):
    put = 0
    for source in sources:
        for here in strips(source.shape[0]):
            values = source[here, :]
            target[put + here.start : put + here.stop, :] = unit_rows(values) if raw else values
        put += source.shape[0]


def nearest(own, near, clusters):
    step = jnp.zeros_like(own)
    for name in range(clusters):
        step = jnp.where(own == name, 2 * near[name] - 1, step)
    other = own + step
    other = jnp.where(other < 0, other + clusters, other)
    return jnp.where(other >= clusters, other - clusters, other)


def as_column(row):
    return jnp.transpose(jnp.broadcast_to(row, (128, row.shape[1])))


def terms(a_unit, b_unit, a_own, a_near, b_own, b_near):
    sim = lax.dot_general(
        a_unit, b_unit, (((1,), (1,)), ((), ())), preferred_element_type=jnp.float32
    )
    wide = sim.shape[1] // 128
    a_own, a_near = jnp.tile(a_own, (1, wide)), jnp.tile(a_near, (1, wide))
    near = jnp.where(a_near == b_own, 0.5, 0.0) + jnp.where(a_own == b_near, 0.5, 0.0)
    return jnp.where(a_own == b_own, 1.0, near) * jnp.exp(16.0 * sim)


def lanes_added(x):
    out = x[:, :128]
    for at in range(128, x.shape[1], 128):
        out = out + x[:, at : at + 128]
    return out


def as_row(x):
    return jnp.sum(jnp.transpose(x), axis=0, keepdims=True)


def sums_kernel(blocks, lists, tasks, kept, added, *refs):
    units = []
    for pieces, *_ in blocks:
        units.append(refs[:pieces])
        refs = refs[pieces:]
    names, refs = refs[:lists], refs[lists:]
    before, sums, refs = refs[:added], refs[added], refs[added + 1 :]
    given, scratch = refs[: len(kept)], list(refs[len(kept) :])
    codes = {}

    def code(block):
        if block not in codes:
            *_, at, row, place = blocks[block]
            here = slice(place, place + units[block].shape[0])
            codes[block] = names[at][row : row + 1, here], names[at][row + 2 : row + 3, here]
        return codes[block]

    for block, (pieces, raw, *_) in enumerate(blocks):
        if raw or pieces > 1:
            target = given[kept.index(block)] if block in kept else scratch.pop(0)
            normalise(units[block], target, raw)
            units[block] = target
        else:
            (units[block],) = units[block]
    sums[...] = before[0][...] if added else jnp.zeros_like(sums)
    for task, block, others in tasks:
        a_own, a_near = [as_column(row) for row in code(block)]
        place = blocks[block][-1]
        for here in strips(units[block].shape[0]):
            total = jnp.zeros((here.stop - here.start, 128), jnp.float32)
            for other in others:
                value = terms(
                    units[block][here, :], units[other][...], a_own[here], a_near[here], *code(other)
                )
                if other == block:
                    row = lax.broadcasted_iota(jnp.int32, value.shape, 0) + here.start
                    same = row == lax.broadcasted_iota(jnp.int32, value.shape, 1)
                    value = jnp.where(same, 0.0, value)
                total = total + lanes_added(value)
            sums[task : task + 1, place + here.start : place + here.stop] += as_row(total)


def row_sums(blocks, names, tasks, label, kept=(), before=None, room=1):
    blocks = [(block if isinstance(block, list) else [block], *rest) for block, *rest in blocks]
    width = blocks[0][0][0].shape[1]
    units = [
        jax.ShapeDtypeStruct((sum(piece.shape[0] for piece in block[0]), width), jnp.bfloat16)
        for block in blocks
    ]
    made = [i for i, block in enumerate(blocks) if block[1] or len(block[0]) > 1]
    scratch = [i for i in made if i not in kept]
    vmem = pl.BlockSpec(memory_space=pltpu.VMEM)
    operands = [piece for block in blocks for piece in block[0]] + names
    operands += [] if before is None else [before]
    sums, *given = pl.pallas_call(
        functools.partial(
            sums_kernel,
            [(len(block[0]), *block[1:]) for block in blocks],
            len(names),
            tasks,
            kept,
            int(before is not None),
        ),
        out_shape=[
            jax.ShapeDtypeStruct((room, names[0].shape[1]), jnp.float32),
            *[units[i] for i in kept],
        ],
        in_specs=[vmem] * len(operands),
        out_specs=[vmem] * (1 + len(kept)),
        scratch_shapes=[pltpu.VMEM(units[i].shape, jnp.bfloat16) for i in scratch],
        compiler_params=pltpu.CompilerParams(vmem_limit_bytes=40 << 20),
        cost_estimate=pl.CostEstimate(flops=0, bytes_accessed=0, transcendentals=0),
        name=label,
    )(*operands)
    return sums, given


def names_kernel(clusters, near, name, other, mine, swapped):
    both = [ref[...] for ref in (name, other)]
    both += [nearest(own, near, clusters) for own in both]
    for at, row in enumerate(both):
        mine[at : at + 1, :] = row
        swapped[at ^ 1 : (at ^ 1) + 1, :] = row


def name_tables(near, name, other):
    table = jax.ShapeDtypeStruct((4, name.shape[1]), jnp.int32)
    vmem = pl.BlockSpec(memory_space=pltpu.VMEM)
    return pl.pallas_call(
        functools.partial(names_kernel, near.shape[0]),
        out_shape=(table, table),
        in_specs=[pl.BlockSpec(memory_space=pltpu.SMEM), vmem, vmem],
        out_specs=(vmem, vmem),
        compiler_params=pltpu.CompilerParams(vmem_limit_bytes=40 << 20),
        cost_estimate=pl.CostEstimate(flops=0, bytes_accessed=0, transcendentals=0),
        name="name_tables",
    )(near, name, other)


def unit_block(rows):
    vmem = pl.BlockSpec(memory_space=pltpu.VMEM)
    return pl.pallas_call(
        lambda source, target: normalise([source], target),
        out_shape=jax.ShapeDtypeStruct(rows.shape, jnp.bfloat16),
        in_specs=[vmem],
        out_specs=vmem,
        compiler_params=pltpu.CompilerParams(vmem_limit_bytes=40 << 20),
        cost_estimate=pl.CostEstimate(flops=0, bytes_accessed=0, transcendentals=0),
        name="unit_rows",
    )(rows)


def per_device(embed, owner, near):
    rows = embed.shape[0]
    chips = lax.axis_size("blk") // 2
    hops = chips // 4
    order = list(range(0, chips, 2)) + list(range(chips - 1, 0, -2))

    def moved(block, target):
        route = []
        for place in range(chips):
            for core in range(2):
                there, to = target(place, core)
                route.append((2 * order[place] + core, 2 * order[there % chips] + to))
        return lax.ppermute(block, "blk", route)

    def other_core(block):
        return moved(block, lambda place, core: (place, 1 - core))

    def onward(place, core):
        return place + 1 - 2 * core, core

    def against(place, core):
        return place - 1 + 2 * core, 1 - core

    def back(distance, half=0):
        return lambda place, core: (place - distance * (1 - 2 * core), core ^ half)

    def split_swap(half):
        return [other_core(part) for part in jnp.split(half, SPLIT)]

    name = owner.reshape(1, rows)
    other_name, other = other_core(name), other_core(embed)
    own_names, swapped_names = name_tables(near, name, other_name)
    side_names, across_names = [own_names], [swapped_names]
    for hop in range(1, hops + 1):
        side_names.append(moved(across_names[-1], against))
        across_names.append(other_core(side_names[-1]))
    total, own = row_sums(
        [(embed, True, 0, 0, 0), (other, True, 0, 1, 0)],
        [own_names],
        ((0, 0, (0, 1)),),
        "own_terms",
        (0,),
    )
    first, second = moved(embed, onward), moved(other, onward)
    first, total, side_names, across_names = lax.optimization_barrier(
        (first, total, side_names, across_names)
    )
    swapped = [None, [split_swap(first)]]
    blocks = [(first, True, 0, 0, 0), (swapped[1][0], True, 1, 0, 0), (own[0], False, 2, 0, 0)]
    sums, units = row_sums(
        blocks,
        [side_names[1], across_names[1], own_names],
        ((0, 0, (1,)), (2, 2, (0, 1))),
        "first_terms",
        (0, 1),
        room=3,
    )
    second, sums = lax.optimization_barrier((second, sums))
    side = [None, [first, unit_block(second)]]
    for hop in range(2, hops + 1):
        halves = side[-1]
        side.append([moved(half, onward) for half in halves])
    across = [None, [swapped[1][0], split_swap(side[1][1])]]
    across += [[split_swap(half) for half in pair] for pair in side[2:hops]]

    inner, theirs = None, 0.0
    for hop in range(1, hops):
        blocks = [(side[hop][0], True, 0, 0, 0), (across[hop][0], True, 1, 0, 0)]
        if hop == 1:
            extra, names = [(own[0], False, 2, 0, 0)], [side_names[1], across_names[1], own_names]
            late = ((0, 0, (3,)), (1, 2, (1, 3)), (2, 4, (2, 3)))
        else:
            extra = [(unit, False, 2, i, 0) for i, unit in enumerate(inner)]
            names = [side_names[hop], across_names[hop], across_names[hop - 1]]
            early = ((0, 0, (1, 2, 3)),)
            late = ((0, 0, (3,)), (1, 2, (1, 3, 4, 5)))
        if hop > 1:
            sums, units = row_sums(
                [*blocks, *extra], names, early, "first_terms", (0, 1), room=3
            )
        blocks = [(unit, False, i, 0, 0) for i, unit in enumerate(units)]
        blocks += [(side[hop][1], False, 0, 1, 0), (across[hop][1], False, 1, 1, 0), *extra]
        sums, (unit,) = row_sums(blocks, names, late, "pair_terms", (3,), before=sums, room=3)
        inner = [units[1], unit]
        returned = moved(sums[:2], back(hop))
        if hop == 1:
            total = total + sums[2:3]
        if hop < hops - 1:
            total, theirs = total + returned[:1], theirs + returned[1:]
    facing, returned, *inner = lax.optimization_barrier((side[hops][0], returned, *inner))
    facing = split_swap(facing)
    total = total + returned[:1] + other_core(theirs + returned[1:])
    names = [side_names[hops], across_names[hops], across_names[hops - 1]]
    blocks = [(side[hops][0], True, 0, 0, 0)]
    blocks += [(unit, False, 2, i, 0) for i, unit in enumerate(inner)]
    tasks = ((0, 0, (2,)), (1, 1, (0,)), (2, 2, (0,)))
    sums, (unit,) = row_sums(blocks, names, tasks, "end_terms", (0,), room=3)
    for half in range(2):
        total = total + moved(sums[1:], back(1 - hops, 1 - half))[half : half + 1]
    blocks = [(unit, False, 0, 0, 0), (facing, True, 1, 0, 0)]
    sums, (facing,) = row_sums(
        blocks, names, ((0, 0, (1,)),), "end_terms", (1,), before=sums[:END_ROOM], room=END_ROOM
    )
    total = total + moved(sums, back(hops))[:1]
    blocks = [(side[hops][1], False, 0, 1, 0), (facing, False, 1, 0, 0), (inner[1], False, 2, 1, 0)]
    sums, _ = row_sums(blocks, names, ((0, 0, (1, 2)),), "end_terms")
    total = total + moved(sums, back(hops, 1))
    return jnp.log1p(total)[0]


def solution(mesh):
    return jax.shard_map(
        per_device,
        mesh=mesh,
        in_specs=(P(("groups", "blk"), None), P(("groups", "blk"), None), P("groups")),
        out_specs=P(("groups", "blk")),
        check_vma=False,
    )
```

```python
import functools

import jax
import jax.numpy as jnp
from jax import lax
from jax.experimental import pallas as pl
from jax.experimental.pallas import tpu as pltpu
from jax.sharding import PartitionSpec as P

STRIP = 256
SPLIT = 2
END_ROOM = 2


def unit_rows(values):
    values = values.astype(jnp.float32)
    width = values.shape[-1]
    scale = lax.rsqrt(jnp.mean(values * values, axis=-1, keepdims=True) + 1e-06) / jnp.sqrt(
        jnp.float32(width)
    )
    return (values * scale).astype(jnp.bfloat16)


def strips(rows):
    return [slice(at, min(at + STRIP, rows)) for at in range(0, rows, STRIP)]


def normalise(sources, target, raw=True):
    put = 0
    for source in sources:
        for here in strips(source.shape[0]):
            values = source[here, :]
            target[put + here.start : put + here.stop, :] = unit_rows(values) if raw else values
        put += source.shape[0]


def nearest(own, near, clusters):
    step = jnp.zeros_like(own)
    for name in range(clusters):
        step = jnp.where(own == name, 2 * near[name] - 1, step)
    other = own + step
    other = jnp.where(other < 0, other + clusters, other)
    return jnp.where(other >= clusters, other - clusters, other)


def as_column(row):
    return jnp.transpose(jnp.broadcast_to(row, (128, row.shape[1])))


def terms(a_unit, b_unit, a_own, a_near, b_own, b_near):
    sim = lax.dot_general(
        a_unit, b_unit, (((1,), (1,)), ((), ())), preferred_element_type=jnp.float32
    )
    wide = sim.shape[1] // 128
    a_own, a_near = jnp.tile(a_own, (1, wide)), jnp.tile(a_near, (1, wide))
    near = jnp.where(a_near == b_own, 0.5, 0.0) + jnp.where(a_own == b_near, 0.5, 0.0)
    return jnp.where(a_own == b_own, 1.0, near) * jnp.exp(16.0 * sim)


def lanes_added(x):
    out = x[:, :128]
    for at in range(128, x.shape[1], 128):
        out = out + x[:, at : at + 128]
    return out


def as_row(x):
    return jnp.sum(jnp.transpose(x), axis=0, keepdims=True)


def sums_kernel(blocks, lists, tasks, kept, added, *refs):
    units = []
    for pieces, *_ in blocks:
        units.append(refs[:pieces])
        refs = refs[pieces:]
    names, refs = refs[:lists], refs[lists:]
    before, sums, refs = refs[:added], refs[added], refs[added + 1 :]
    given, scratch = refs[: len(kept)], list(refs[len(kept) :])
    codes = {}

    def code(block):
        if block not in codes:
            *_, at, row, place = blocks[block]
            here = slice(place, place + units[block].shape[0])
            codes[block] = names[at][row : row + 1, here], names[at][row + 2 : row + 3, here]
        return codes[block]

    for block, (pieces, raw, *_) in enumerate(blocks):
        if raw or pieces > 1:
            target = given[kept.index(block)] if block in kept else scratch.pop(0)
            normalise(units[block], target, raw)
            units[block] = target
        else:
            (units[block],) = units[block]
    sums[...] = before[0][...] if added else jnp.zeros_like(sums)
    for task, block, others in tasks:
        a_own, a_near = [as_column(row) for row in code(block)]
        place = blocks[block][-1]
        here_all = strips(units[block].shape[0])
        totals = [jnp.zeros((here.stop - here.start, 128), jnp.float32) for here in here_all]
        for other in others:
            b_own, b_near = code(other)
            for there in strips(units[other].shape[0]):
                for at, here in enumerate(here_all):
                    value = terms(
                        units[block][here, :],
                        units[other][there, :],
                        a_own[here],
                        a_near[here],
                        b_own[:, there],
                        b_near[:, there],
                    )
                    if other == block and here == there:
                        row = lax.broadcasted_iota(jnp.int32, value.shape, 0)
                        same = row == lax.broadcasted_iota(jnp.int32, value.shape, 1)
                        value = jnp.where(same, 0.0, value)
                    totals[at] = totals[at] + lanes_added(value)
        for here, total in zip(here_all, totals):
            sums[task : task + 1, place + here.start : place + here.stop] += as_row(total)


def row_sums(blocks, names, tasks, label, kept=(), before=None, room=1):
    blocks = [(block if isinstance(block, list) else [block], *rest) for block, *rest in blocks]
    width = blocks[0][0][0].shape[1]
    units = [
        jax.ShapeDtypeStruct((sum(piece.shape[0] for piece in block[0]), width), jnp.bfloat16)
        for block in blocks
    ]
    made = [i for i, block in enumerate(blocks) if block[1] or len(block[0]) > 1]
    scratch = [i for i in made if i not in kept]
    vmem = pl.BlockSpec(memory_space=pltpu.VMEM)
    operands = [piece for block in blocks for piece in block[0]] + names
    operands += [] if before is None else [before]
    sums, *given = pl.pallas_call(
        functools.partial(
            sums_kernel,
            [(len(block[0]), *block[1:]) for block in blocks],
            len(names),
            tasks,
            kept,
            int(before is not None),
        ),
        out_shape=[
            jax.ShapeDtypeStruct((room, names[0].shape[1]), jnp.float32),
            *[units[i] for i in kept],
        ],
        in_specs=[vmem] * len(operands),
        out_specs=[vmem] * (1 + len(kept)),
        scratch_shapes=[pltpu.VMEM(units[i].shape, jnp.bfloat16) for i in scratch],
        compiler_params=pltpu.CompilerParams(vmem_limit_bytes=40 << 20),
        cost_estimate=pl.CostEstimate(flops=0, bytes_accessed=0, transcendentals=0),
        name=label,
    )(*operands)
    return sums, given


def names_kernel(clusters, near, name, other, mine, swapped):
    both = [ref[...] for ref in (name, other)]
    both += [nearest(own, near, clusters) for own in both]
    for at, row in enumerate(both):
        mine[at : at + 1, :] = row
        swapped[at ^ 1 : (at ^ 1) + 1, :] = row


def name_tables(near, name, other):
    table = jax.ShapeDtypeStruct((4, name.shape[1]), jnp.int32)
    vmem = pl.BlockSpec(memory_space=pltpu.VMEM)
    return pl.pallas_call(
        functools.partial(names_kernel, near.shape[0]),
        out_shape=(table, table),
        in_specs=[pl.BlockSpec(memory_space=pltpu.SMEM), vmem, vmem],
        out_specs=(vmem, vmem),
        compiler_params=pltpu.CompilerParams(vmem_limit_bytes=40 << 20),
        cost_estimate=pl.CostEstimate(flops=0, bytes_accessed=0, transcendentals=0),
        name="name_tables",
    )(near, name, other)


def unit_block(rows):
    vmem = pl.BlockSpec(memory_space=pltpu.VMEM)
    return pl.pallas_call(
        lambda source, target: normalise([source], target),
        out_shape=jax.ShapeDtypeStruct(rows.shape, jnp.bfloat16),
        in_specs=[vmem],
        out_specs=vmem,
        compiler_params=pltpu.CompilerParams(vmem_limit_bytes=40 << 20),
        cost_estimate=pl.CostEstimate(flops=0, bytes_accessed=0, transcendentals=0),
        name="unit_rows",
    )(rows)


def per_device(embed, owner, near):
    rows = embed.shape[0]
    chips = lax.axis_size("blk") // 2
    hops = chips // 4
    order = list(range(0, chips, 2)) + list(range(chips - 1, 0, -2))

    def moved(block, target):
        route = []
        for place in range(chips):
            for core in range(2):
                there, to = target(place, core)
                route.append((2 * order[place] + core, 2 * order[there % chips] + to))
        return lax.ppermute(block, "blk", route)

    def other_core(block):
        return moved(block, lambda place, core: (place, 1 - core))

    def onward(place, core):
        return place + 1 - 2 * core, core

    def against(place, core):
        return place - 1 + 2 * core, 1 - core

    def back(distance, half=0):
        return lambda place, core: (place - distance * (1 - 2 * core), core ^ half)

    def split_swap(half):
        return [other_core(part) for part in jnp.split(half, SPLIT)]

    name = owner.reshape(1, rows)
    other_name, other = other_core(name), other_core(embed)
    own_names, swapped_names = name_tables(near, name, other_name)
    side_names, across_names = [own_names], [swapped_names]
    for hop in range(1, hops + 1):
        side_names.append(moved(across_names[-1], against))
        across_names.append(other_core(side_names[-1]))
    total, own = row_sums(
        [(embed, True, 0, 0, 0), (other, True, 0, 1, 0)],
        [own_names],
        ((0, 0, (0, 1)),),
        "own_terms",
        (0,),
    )
    first, second = moved(embed, onward), moved(other, onward)
    first, total, side_names, across_names = lax.optimization_barrier(
        (first, total, side_names, across_names)
    )
    swapped = [None, [split_swap(first)]]
    blocks = [(first, True, 0, 0, 0), (swapped[1][0], True, 1, 0, 0), (own[0], False, 2, 0, 0)]
    sums, units = row_sums(
        blocks,
        [side_names[1], across_names[1], own_names],
        ((0, 0, (1,)), (2, 2, (0, 1))),
        "first_terms",
        (0, 1),
        room=3,
    )
    second, sums = lax.optimization_barrier((second, sums))
    side = [None, [first, unit_block(second)]]
    for hop in range(2, hops + 1):
        halves = side[-1]
        side.append([moved(half, onward) for half in halves])
    across = [None, [swapped[1][0], split_swap(side[1][1])]]
    across += [[split_swap(half) for half in pair] for pair in side[2:hops]]

    inner, theirs = None, 0.0
    for hop in range(1, hops):
        blocks = [(side[hop][0], True, 0, 0, 0), (across[hop][0], True, 1, 0, 0)]
        if hop == 1:
            extra, names = [(own[0], False, 2, 0, 0)], [side_names[1], across_names[1], own_names]
            late = ((0, 0, (3,)), (1, 2, (1, 3)), (2, 4, (2, 3)))
        else:
            extra = [(unit, False, 2, i, 0) for i, unit in enumerate(inner)]
            names = [side_names[hop], across_names[hop], across_names[hop - 1]]
            early = ((0, 0, (1, 2, 3)),)
            late = ((0, 0, (3,)), (1, 2, (1, 3, 4, 5)))
        if hop > 1:
            sums, units = row_sums(
                [*blocks, *extra], names, early, "first_terms", (0, 1), room=3
            )
        blocks = [(unit, False, i, 0, 0) for i, unit in enumerate(units)]
        blocks += [(side[hop][1], False, 0, 1, 0), (across[hop][1], False, 1, 1, 0), *extra]
        sums, (unit,) = row_sums(blocks, names, late, "pair_terms", (3,), before=sums, room=3)
        inner = [units[1], unit]
        returned = moved(sums[:2], back(hop))
        if hop == 1:
            total = total + sums[2:3]
        if hop < hops - 1:
            total, theirs = total + returned[:1], theirs + returned[1:]
    facing, returned, *inner = lax.optimization_barrier((side[hops][0], returned, *inner))
    facing = split_swap(facing)
    total = total + returned[:1] + other_core(theirs + returned[1:])
    names = [side_names[hops], across_names[hops], across_names[hops - 1]]
    blocks = [(side[hops][0], True, 0, 0, 0)]
    blocks += [(unit, False, 2, i, 0) for i, unit in enumerate(inner)]
    tasks = ((0, 0, (2,)), (1, 1, (0,)), (2, 2, (0,)))
    sums, (unit,) = row_sums(blocks, names, tasks, "end_terms", (0,), room=3)
    for half in range(2):
        total = total + moved(sums[1:], back(1 - hops, 1 - half))[half : half + 1]
    blocks = [(unit, False, 0, 0, 0), (facing, True, 1, 0, 0)]
    sums, (facing,) = row_sums(
        blocks, names, ((0, 0, (1,)),), "end_terms", (1,), before=sums[:END_ROOM], room=END_ROOM
    )
    total = total + moved(sums, back(hops))[:1]
    blocks = [(side[hops][1], False, 0, 1, 0), (facing, False, 1, 0, 0), (inner[1], False, 2, 1, 0)]
    sums, _ = row_sums(blocks, names, ((0, 0, (1, 2)),), "end_terms")
    total = total + moved(sums, back(hops, 1))
    return jnp.log1p(total)[0]


def solution(mesh):
    return jax.shard_map(
        per_device,
        mesh=mesh,
        in_specs=(P(("groups", "blk"), None), P(("groups", "blk"), None), P("groups")),
        out_specs=P(("groups", "blk")),
        check_vma=False,
    )
```

```python
import functools

import jax
import jax.numpy as jnp
from jax import lax
from jax.experimental import pallas as pl
from jax.experimental.pallas import tpu as pltpu
from jax.sharding import PartitionSpec as P

STRIP = 256
SPLIT = 2
END_ROOM = 2


def unit_rows(values):
    values = values.astype(jnp.float32)
    width = values.shape[-1]
    scale = lax.rsqrt(jnp.mean(values * values, axis=-1, keepdims=True) + 1e-06) / jnp.sqrt(
        jnp.float32(width)
    )
    return (values * scale).astype(jnp.bfloat16)


def strips(rows):
    return [slice(at, min(at + STRIP, rows)) for at in range(0, rows, STRIP)]


def normalise(sources, target, raw=True):
    put = 0
    for source in sources:
        for here in strips(source.shape[0]):
            values = source[here, :]
            target[put + here.start : put + here.stop, :] = unit_rows(values) if raw else values
        put += source.shape[0]


def nearest(own, near, clusters):
    step = jnp.zeros_like(own)
    for name in range(clusters):
        step = jnp.where(own == name, 2 * near[name] - 1, step)
    other = own + step
    other = jnp.where(other < 0, other + clusters, other)
    return jnp.where(other >= clusters, other - clusters, other)


def as_column(row):
    return jnp.transpose(jnp.broadcast_to(row, (128, row.shape[1])))


def weights(a_own, a_near, b_own, b_near):
    wide = b_own.shape[1] // 128
    a_own, a_near = jnp.tile(a_own, (1, wide)), jnp.tile(a_near, (1, wide))
    near = jnp.where(a_near == b_own, 0.5, 0.0) + jnp.where(a_own == b_near, 0.5, 0.0)
    return jnp.where(a_own == b_own, 1.0, near)


def exponentials(a_unit, b_unit):
    sim = lax.dot_general(
        a_unit, b_unit, (((1,), (1,)), ((), ())), preferred_element_type=jnp.float32
    )
    return jnp.exp(16.0 * sim)


def terms(a_unit, b_unit, a_own, a_near, b_own, b_near):
    return weights(a_own, a_near, b_own, b_near) * exponentials(a_unit, b_unit)


def lanes_added(x):
    out = x[:, :128]
    for at in range(128, x.shape[1], 128):
        out = out + x[:, at : at + 128]
    return out


def as_row(x):
    return jnp.sum(jnp.transpose(x), axis=0, keepdims=True)


def sums_kernel(blocks, lists, tasks, kept, added, *refs):
    units = []
    for pieces, *_ in blocks:
        units.append(refs[:pieces])
        refs = refs[pieces:]
    names, refs = refs[:lists], refs[lists:]
    before, sums, refs = refs[:added], refs[added], refs[added + 1 :]
    given, scratch = refs[: len(kept)], list(refs[len(kept) :])
    codes = {}

    def code(block):
        if block not in codes:
            *_, at, row, place = blocks[block]
            here = slice(place, place + units[block].shape[0])
            codes[block] = names[at][row : row + 1, here], names[at][row + 2 : row + 3, here]
        return codes[block]

    for block, (pieces, raw, *_) in enumerate(blocks):
        if raw or pieces > 1:
            target = given[kept.index(block)] if block in kept else scratch.pop(0)
            normalise(units[block], target, raw)
            units[block] = target
        else:
            (units[block],) = units[block]
    sums[...] = before[0][...] if added else jnp.zeros_like(sums)
    for task, block, others in tasks:
        a_own, a_near = [as_column(row) for row in code(block)]
        place = blocks[block][-1]
        here_all = strips(units[block].shape[0])
        totals = [jnp.zeros((here.stop - here.start, 128), jnp.float32) for here in here_all]
        for other in others:
            b_own, b_near = code(other)
            for there in strips(units[other].shape[0]):
                for at, here in enumerate(here_all):
                    value = terms(
                        units[block][here, :],
                        units[other][there, :],
                        a_own[here],
                        a_near[here],
                        b_own[:, there],
                        b_near[:, there],
                    )
                    if other == block and here == there:
                        row = lax.broadcasted_iota(jnp.int32, value.shape, 0)
                        same = row == lax.broadcasted_iota(jnp.int32, value.shape, 1)
                        value = jnp.where(same, 0.0, value)
                    totals[at] = totals[at] + lanes_added(value)
        for here, total in zip(here_all, totals):
            sums[task : task + 1, place + here.start : place + here.stop] += as_row(total)


def row_sums(blocks, names, tasks, label, kept=(), before=None, room=1):
    blocks = [(block if isinstance(block, list) else [block], *rest) for block, *rest in blocks]
    width = blocks[0][0][0].shape[1]
    units = [
        jax.ShapeDtypeStruct((sum(piece.shape[0] for piece in block[0]), width), jnp.bfloat16)
        for block in blocks
    ]
    made = [i for i, block in enumerate(blocks) if block[1] or len(block[0]) > 1]
    scratch = [i for i in made if i not in kept]
    vmem = pl.BlockSpec(memory_space=pltpu.VMEM)
    operands = [piece for block in blocks for piece in block[0]] + names
    operands += [] if before is None else [before]
    sums, *given = pl.pallas_call(
        functools.partial(
            sums_kernel,
            [(len(block[0]), *block[1:]) for block in blocks],
            len(names),
            tasks,
            kept,
            int(before is not None),
        ),
        out_shape=[
            jax.ShapeDtypeStruct((room, names[0].shape[1]), jnp.float32),
            *[units[i] for i in kept],
        ],
        in_specs=[vmem] * len(operands),
        out_specs=[vmem] * (1 + len(kept)),
        scratch_shapes=[pltpu.VMEM(units[i].shape, jnp.bfloat16) for i in scratch],
        compiler_params=pltpu.CompilerParams(vmem_limit_bytes=40 << 20),
        cost_estimate=pl.CostEstimate(flops=0, bytes_accessed=0, transcendentals=0),
        name=label,
    )(*operands)
    return sums, given


def names_kernel(clusters, near, name, other, mine, swapped):
    both = [ref[...] for ref in (name, other)]
    both += [nearest(own, near, clusters) for own in both]
    for at, row in enumerate(both):
        mine[at : at + 1, :] = row
        swapped[at ^ 1 : (at ^ 1) + 1, :] = row


def name_tables(near, name, other):
    table = jax.ShapeDtypeStruct((4, name.shape[1]), jnp.int32)
    vmem = pl.BlockSpec(memory_space=pltpu.VMEM)
    return pl.pallas_call(
        functools.partial(names_kernel, near.shape[0]),
        out_shape=(table, table),
        in_specs=[pl.BlockSpec(memory_space=pltpu.SMEM), vmem, vmem],
        out_specs=(vmem, vmem),
        compiler_params=pltpu.CompilerParams(vmem_limit_bytes=40 << 20),
        cost_estimate=pl.CostEstimate(flops=0, bytes_accessed=0, transcendentals=0),
        name="name_tables",
    )(near, name, other)


def unit_block(rows):
    vmem = pl.BlockSpec(memory_space=pltpu.VMEM)
    return pl.pallas_call(
        lambda source, target: normalise([source], target),
        out_shape=jax.ShapeDtypeStruct(rows.shape, jnp.bfloat16),
        in_specs=[vmem],
        out_specs=vmem,
        compiler_params=pltpu.CompilerParams(vmem_limit_bytes=40 << 20),
        cost_estimate=pl.CostEstimate(flops=0, bytes_accessed=0, transcendentals=0),
        name="unit_rows",
    )(rows)


def weights_kernel(a_names, *refs):
    b_names, result = refs[:-1], refs[-1]
    a_own, a_near = [as_column(a_names[row : row + 1, :]) for row in (1, 3)]
    rows = a_names.shape[1]
    for at, names in enumerate(b_names):
        there = slice(at * rows, (at + 1) * rows)
        for here in strips(rows):
            value = weights(a_own[here], a_near[here], names[at : at + 1, :], names[at + 2 : at + 3, :])
            result[here, there] = value.astype(jnp.bfloat16)


def last_kernel(a, *refs):
    others, weight, sums = refs[:-2], refs[-2], refs[-1]
    rows = a.shape[0]
    totals = [jnp.zeros((here.stop - here.start, 128), jnp.float32) for here in strips(rows)]
    for number, other in enumerate(others):
        for there in strips(rows):
            column = slice(number * rows + there.start, number * rows + there.stop)
            for at, here in enumerate(strips(rows)):
                value = exponentials(a[here, :], other[there, :])
                value = weight[here, column].astype(jnp.float32) * value
                totals[at] = totals[at] + lanes_added(value)
    for here, total in zip(strips(rows), totals):
        sums[:, here] = as_row(total)


def in_vmem(kernel, shape, dtype, label, *operands):
    vmem = pl.BlockSpec(memory_space=pltpu.VMEM)
    return pl.pallas_call(
        kernel,
        out_shape=jax.ShapeDtypeStruct(shape, dtype),
        in_specs=[vmem] * len(operands),
        out_specs=vmem,
        compiler_params=pltpu.CompilerParams(vmem_limit_bytes=40 << 20),
        cost_estimate=pl.CostEstimate(flops=0, bytes_accessed=0, transcendentals=0),
        name=label,
    )(*operands)


def per_device(embed, owner, near):
    rows = embed.shape[0]
    chips = lax.axis_size("blk") // 2
    hops = chips // 4
    order = list(range(0, chips, 2)) + list(range(chips - 1, 0, -2))

    def moved(block, target):
        route = []
        for place in range(chips):
            for core in range(2):
                there, to = target(place, core)
                route.append((2 * order[place] + core, 2 * order[there % chips] + to))
        return lax.ppermute(block, "blk", route)

    def other_core(block):
        return moved(block, lambda place, core: (place, 1 - core))

    def onward(place, core):
        return place + 1 - 2 * core, core

    def against(place, core):
        return place - 1 + 2 * core, 1 - core

    def back(distance, half=0):
        return lambda place, core: (place - distance * (1 - 2 * core), core ^ half)

    def split_swap(half):
        return [other_core(part) for part in jnp.split(half, SPLIT)]

    name = owner.reshape(1, rows)
    other_name, other = other_core(name), other_core(embed)
    own_names, swapped_names = name_tables(near, name, other_name)
    side_names, across_names = [own_names], [swapped_names]
    for hop in range(1, hops + 1):
        side_names.append(moved(across_names[-1], against))
        across_names.append(other_core(side_names[-1]))
    total, own = row_sums(
        [(embed, True, 0, 0, 0), (other, True, 0, 1, 0)],
        [own_names],
        ((0, 0, (0, 1)),),
        "own_terms",
        (0,),
    )
    first, second = moved(embed, onward), moved(other, onward)
    first, total, side_names, across_names = lax.optimization_barrier(
        (first, total, side_names, across_names)
    )
    swapped = [None, [split_swap(first)]]
    blocks = [(first, True, 0, 0, 0), (swapped[1][0], True, 1, 0, 0), (own[0], False, 2, 0, 0)]
    sums, units = row_sums(
        blocks,
        [side_names[1], across_names[1], own_names],
        ((0, 0, (1,)), (2, 2, (0, 1))),
        "first_terms",
        (0, 1),
        room=3,
    )
    second, sums = lax.optimization_barrier((second, sums))
    side = [None, [first, unit_block(second)]]
    for hop in range(2, hops + 1):
        halves = side[-1]
        side.append([moved(half, onward) for half in halves])
    across = [None, [swapped[1][0], split_swap(side[1][1])]]
    across += [[split_swap(half) for half in pair] for pair in side[2:hops]]

    inner, theirs = None, 0.0
    for hop in range(1, hops):
        blocks = [(side[hop][0], True, 0, 0, 0), (across[hop][0], True, 1, 0, 0)]
        if hop == 1:
            extra, names = [(own[0], False, 2, 0, 0)], [side_names[1], across_names[1], own_names]
            late = ((0, 0, (3,)), (1, 2, (1, 3)), (2, 4, (2, 3)))
        else:
            extra = [(unit, False, 2, i, 0) for i, unit in enumerate(inner)]
            names = [side_names[hop], across_names[hop], across_names[hop - 1]]
            early = ((0, 0, (1, 2, 3)),)
            late = ((0, 0, (3,)), (1, 2, (1, 3, 4, 5)))
        if hop > 1:
            sums, units = row_sums(
                [*blocks, *extra], names, early, "first_terms", (0, 1), room=3
            )
        blocks = [(unit, False, i, 0, 0) for i, unit in enumerate(units)]
        blocks += [(side[hop][1], False, 0, 1, 0), (across[hop][1], False, 1, 1, 0), *extra]
        sums, (unit,) = row_sums(blocks, names, late, "pair_terms", (3,), before=sums, room=3)
        inner = [units[1], unit]
        returned = moved(sums[:2], back(hop))
        if hop == 1:
            total = total + sums[2:3]
        if hop < hops - 1:
            total, theirs = total + returned[:1], theirs + returned[1:]
    facing, returned, *inner = lax.optimization_barrier((side[hops][0], returned, *inner))
    facing = split_swap(facing)
    total = total + returned[:1] + other_core(theirs + returned[1:])
    names = [side_names[hops], across_names[hops], across_names[hops - 1]]
    blocks = [(side[hops][0], True, 0, 0, 0)]
    blocks += [(unit, False, 2, i, 0) for i, unit in enumerate(inner)]
    tasks = ((0, 0, (2,)), (1, 1, (0,)), (2, 2, (0,)))
    sums, (unit,) = row_sums(blocks, names, tasks, "end_terms", (0,), room=3)
    for half in range(2):
        total = total + moved(sums[1:], back(1 - hops, 1 - half))[half : half + 1]
    blocks = [(unit, False, 0, 0, 0), (facing, True, 1, 0, 0)]
    sums, (facing,) = row_sums(
        blocks, names, ((0, 0, (1,)),), "end_terms", (1,), before=sums[:END_ROOM], room=END_ROOM
    )
    total = total + moved(sums, back(hops))[:1]
    weight = in_vmem(weights_kernel, (rows, 2 * rows), jnp.bfloat16, "end_weights", *names)
    sums = in_vmem(
        last_kernel, (1, rows), jnp.float32, "last_terms", side[hops][1], facing, inner[1], weight
    )
    total = total + moved(sums, back(hops, 1))
    return jnp.log1p(total)[0]


def solution(mesh):
    return jax.shard_map(
        per_device,
        mesh=mesh,
        in_specs=(P(("groups", "blk"), None), P(("groups", "blk"), None), P("groups")),
        out_specs=P(("groups", "blk")),
        check_vma=False,
    )
```

```python
import functools

import jax
import jax.numpy as jnp
from jax import lax
from jax.experimental import pallas as pl
from jax.experimental.pallas import tpu as pltpu
from jax.sharding import PartitionSpec as P

STRIP = 512
SPLIT = 2
END_ROOM = 2


def unit_rows(values):
    values = values.astype(jnp.float32)
    width = values.shape[-1]
    scale = lax.rsqrt(jnp.mean(values * values, axis=-1, keepdims=True) + 1e-06) / jnp.sqrt(
        jnp.float32(width)
    )
    return (values * scale).astype(jnp.bfloat16)


def strips(rows):
    return [slice(at, min(at + STRIP, rows)) for at in range(0, rows, STRIP)]


def normalise(sources, target, raw=True):
    put = 0
    for source in sources:
        for here in strips(source.shape[0]):
            values = source[here, :]
            target[put + here.start : put + here.stop, :] = unit_rows(values) if raw else values
        put += source.shape[0]


def nearest(own, near, clusters):
    step = jnp.zeros_like(own)
    for name in range(clusters):
        step = jnp.where(own == name, 2 * near[name] - 1, step)
    other = own + step
    other = jnp.where(other < 0, other + clusters, other)
    return jnp.where(other >= clusters, other - clusters, other)


def as_column(row):
    return jnp.transpose(jnp.broadcast_to(row, (128, row.shape[1])))


def weights(a_own, a_near, b_own, b_near):
    wide = b_own.shape[1] // 128
    a_own, a_near = jnp.tile(a_own, (1, wide)), jnp.tile(a_near, (1, wide))
    near = jnp.where(a_near == b_own, 0.5, 0.0) + jnp.where(a_own == b_near, 0.5, 0.0)
    return jnp.where(a_own == b_own, 1.0, near)


def exponentials(a_unit, b_unit):
    sim = lax.dot_general(
        a_unit, b_unit, (((1,), (1,)), ((), ())), preferred_element_type=jnp.float32
    )
    return jnp.exp(16.0 * sim)


def terms(a_unit, b_unit, a_own, a_near, b_own, b_near):
    return weights(a_own, a_near, b_own, b_near) * exponentials(a_unit, b_unit)


def lanes_added(x):
    out = x[:, :128]
    for at in range(128, x.shape[1], 128):
        out = out + x[:, at : at + 128]
    return out


def as_row(x):
    return jnp.sum(jnp.transpose(x), axis=0, keepdims=True)


def sums_kernel(blocks, lists, tasks, kept, added, *refs):
    units = []
    for pieces, *_ in blocks:
        units.append(refs[:pieces])
        refs = refs[pieces:]
    names, refs = refs[:lists], refs[lists:]
    before, sums, refs = refs[:added], refs[added], refs[added + 1 :]
    given, scratch = refs[: len(kept)], list(refs[len(kept) :])
    codes = {}

    def code(block):
        if block not in codes:
            *_, at, row, place = blocks[block]
            here = slice(place, place + units[block].shape[0])
            codes[block] = names[at][row : row + 1, here], names[at][row + 2 : row + 3, here]
        return codes[block]

    for block, (pieces, raw, *_) in enumerate(blocks):
        if raw or pieces > 1:
            target = given[kept.index(block)] if block in kept else scratch.pop(0)
            normalise(units[block], target, raw)
            units[block] = target
        else:
            (units[block],) = units[block]
    sums[...] = before[0][...] if added else jnp.zeros_like(sums)
    for task, block, others in tasks:
        a_own, a_near = [as_column(row) for row in code(block)]
        place = blocks[block][-1]
        here_all = strips(units[block].shape[0])
        totals = [jnp.zeros((here.stop - here.start, 128), jnp.float32) for here in here_all]
        for other in others:
            b_own, b_near = code(other)
            for there in strips(units[other].shape[0]):
                for at, here in enumerate(here_all):
                    value = terms(
                        units[block][here, :],
                        units[other][there, :],
                        a_own[here],
                        a_near[here],
                        b_own[:, there],
                        b_near[:, there],
                    )
                    if other == block and here == there:
                        row = lax.broadcasted_iota(jnp.int32, value.shape, 0)
                        same = row == lax.broadcasted_iota(jnp.int32, value.shape, 1)
                        value = jnp.where(same, 0.0, value)
                    totals[at] = totals[at] + lanes_added(value)
        for here, total in zip(here_all, totals):
            sums[task : task + 1, place + here.start : place + here.stop] += as_row(total)


def row_sums(blocks, names, tasks, label, kept=(), before=None, room=1):
    blocks = [(block if isinstance(block, list) else [block], *rest) for block, *rest in blocks]
    width = blocks[0][0][0].shape[1]
    units = [
        jax.ShapeDtypeStruct((sum(piece.shape[0] for piece in block[0]), width), jnp.bfloat16)
        for block in blocks
    ]
    made = [i for i, block in enumerate(blocks) if block[1] or len(block[0]) > 1]
    scratch = [i for i in made if i not in kept]
    vmem = pl.BlockSpec(memory_space=pltpu.VMEM)
    operands = [piece for block in blocks for piece in block[0]] + names
    operands += [] if before is None else [before]
    sums, *given = pl.pallas_call(
        functools.partial(
            sums_kernel,
            [(len(block[0]), *block[1:]) for block in blocks],
            len(names),
            tasks,
            kept,
            int(before is not None),
        ),
        out_shape=[
            jax.ShapeDtypeStruct((room, names[0].shape[1]), jnp.float32),
            *[units[i] for i in kept],
        ],
        in_specs=[vmem] * len(operands),
        out_specs=[vmem] * (1 + len(kept)),
        scratch_shapes=[pltpu.VMEM(units[i].shape, jnp.bfloat16) for i in scratch],
        compiler_params=pltpu.CompilerParams(vmem_limit_bytes=40 << 20),
        cost_estimate=pl.CostEstimate(flops=0, bytes_accessed=0, transcendentals=0),
        name=label,
    )(*operands)
    return sums, given


def names_kernel(clusters, near, name, other, mine, swapped):
    both = [ref[...] for ref in (name, other)]
    both += [nearest(own, near, clusters) for own in both]
    for at, row in enumerate(both):
        mine[at : at + 1, :] = row
        swapped[at ^ 1 : (at ^ 1) + 1, :] = row


def name_tables(near, name, other):
    table = jax.ShapeDtypeStruct((4, name.shape[1]), jnp.int32)
    vmem = pl.BlockSpec(memory_space=pltpu.VMEM)
    return pl.pallas_call(
        functools.partial(names_kernel, near.shape[0]),
        out_shape=(table, table),
        in_specs=[pl.BlockSpec(memory_space=pltpu.SMEM), vmem, vmem],
        out_specs=(vmem, vmem),
        compiler_params=pltpu.CompilerParams(vmem_limit_bytes=40 << 20),
        cost_estimate=pl.CostEstimate(flops=0, bytes_accessed=0, transcendentals=0),
        name="name_tables",
    )(near, name, other)


def unit_block(rows):
    vmem = pl.BlockSpec(memory_space=pltpu.VMEM)
    return pl.pallas_call(
        lambda source, target: normalise([source], target),
        out_shape=jax.ShapeDtypeStruct(rows.shape, jnp.bfloat16),
        in_specs=[vmem],
        out_specs=vmem,
        compiler_params=pltpu.CompilerParams(vmem_limit_bytes=40 << 20),
        cost_estimate=pl.CostEstimate(flops=0, bytes_accessed=0, transcendentals=0),
        name="unit_rows",
    )(rows)


def weights_kernel(a_names, *refs):
    b_names, result = refs[:-1], refs[-1]
    a_own, a_near = [as_column(a_names[row : row + 1, :]) for row in (1, 3)]
    rows = a_names.shape[1]
    for at, names in enumerate(b_names):
        there = slice(at * rows, (at + 1) * rows)
        for here in strips(rows):
            value = weights(a_own[here], a_near[here], names[at : at + 1, :], names[at + 2 : at + 3, :])
            result[here, there] = value.astype(jnp.bfloat16)


def last_kernel(a, *refs):
    others, weight, sums = refs[:-2], refs[-2], refs[-1]
    rows = a.shape[0]
    totals = [jnp.zeros((here.stop - here.start, 128), jnp.float32) for here in strips(rows)]
    for number, other in enumerate(others):
        for there in strips(rows):
            column = slice(number * rows + there.start, number * rows + there.stop)
            for at, here in enumerate(strips(rows)):
                value = exponentials(a[here, :], other[there, :])
                value = weight[here, column].astype(jnp.float32) * value
                totals[at] = totals[at] + lanes_added(value)
    for here, total in zip(strips(rows), totals):
        sums[:, here] = as_row(total)


def in_vmem(kernel, shape, dtype, label, *operands):
    vmem = pl.BlockSpec(memory_space=pltpu.VMEM)
    return pl.pallas_call(
        kernel,
        out_shape=jax.ShapeDtypeStruct(shape, dtype),
        in_specs=[vmem] * len(operands),
        out_specs=vmem,
        compiler_params=pltpu.CompilerParams(vmem_limit_bytes=40 << 20),
        cost_estimate=pl.CostEstimate(flops=0, bytes_accessed=0, transcendentals=0),
        name=label,
    )(*operands)


def per_device(embed, owner, near):
    rows = embed.shape[0]
    chips = lax.axis_size("blk") // 2
    hops = chips // 4
    order = list(range(0, chips, 2)) + list(range(chips - 1, 0, -2))

    def moved(block, target):
        route = []
        for place in range(chips):
            for core in range(2):
                there, to = target(place, core)
                route.append((2 * order[place] + core, 2 * order[there % chips] + to))
        return lax.ppermute(block, "blk", route)

    def other_core(block):
        return moved(block, lambda place, core: (place, 1 - core))

    def onward(place, core):
        return place + 1 - 2 * core, core

    def against(place, core):
        return place - 1 + 2 * core, 1 - core

    def back(distance, half=0):
        return lambda place, core: (place - distance * (1 - 2 * core), core ^ half)

    def split_swap(half):
        return [other_core(part) for part in jnp.split(half, SPLIT)]

    name = owner.reshape(1, rows)
    other_name, other = other_core(name), other_core(embed)
    own_names, swapped_names = name_tables(near, name, other_name)
    side_names, across_names = [own_names], [swapped_names]
    for hop in range(1, hops + 1):
        side_names.append(moved(across_names[-1], against))
        across_names.append(other_core(side_names[-1]))
    total, own = row_sums(
        [(embed, True, 0, 0, 0), (other, True, 0, 1, 0)],
        [own_names],
        ((0, 0, (0, 1)),),
        "own_terms",
        (0,),
    )
    first, second = moved(embed, onward), moved(other, onward)
    first, total, side_names, across_names = lax.optimization_barrier(
        (first, total, side_names, across_names)
    )
    swapped = [None, [split_swap(first)]]
    blocks = [(first, True, 0, 0, 0), (swapped[1][0], True, 1, 0, 0), (own[0], False, 2, 0, 0)]
    sums, units = row_sums(
        blocks,
        [side_names[1], across_names[1], own_names],
        ((0, 0, (1,)), (2, 2, (0, 1))),
        "first_terms",
        (0, 1),
        room=3,
    )
    second, sums = lax.optimization_barrier((second, sums))
    side = [None, [first, unit_block(second)]]
    for hop in range(2, hops + 1):
        halves = side[-1]
        side.append([moved(half, onward) for half in halves])
    across = [None, [swapped[1][0], split_swap(side[1][1])]]
    across += [[split_swap(half) for half in pair] for pair in side[2:hops]]

    inner, theirs = None, 0.0
    for hop in range(1, hops):
        blocks = [(side[hop][0], True, 0, 0, 0), (across[hop][0], True, 1, 0, 0)]
        if hop == 1:
            extra, names = [(own[0], False, 2, 0, 0)], [side_names[1], across_names[1], own_names]
            late = ((0, 0, (3,)), (1, 2, (1, 3)), (2, 4, (2, 3)))
        else:
            extra = [(unit, False, 2, i, 0) for i, unit in enumerate(inner)]
            names = [side_names[hop], across_names[hop], across_names[hop - 1]]
            early = ((0, 0, (1, 2, 3)),)
            late = ((0, 0, (3,)), (1, 2, (1, 3, 4, 5)))
        if hop > 1:
            sums, units = row_sums(
                [*blocks, *extra], names, early, "first_terms", (0, 1), room=3
            )
        blocks = [(unit, False, i, 0, 0) for i, unit in enumerate(units)]
        blocks += [(side[hop][1], False, 0, 1, 0), (across[hop][1], False, 1, 1, 0), *extra]
        sums, (unit,) = row_sums(blocks, names, late, "pair_terms", (3,), before=sums, room=3)
        inner = [units[1], unit]
        returned = moved(sums[:2], back(hop))
        if hop == 1:
            total = total + sums[2:3]
        if hop < hops - 1:
            total, theirs = total + returned[:1], theirs + returned[1:]
    facing, returned, *inner = lax.optimization_barrier((side[hops][0], returned, *inner))
    facing = split_swap(facing)
    total = total + returned[:1] + other_core(theirs + returned[1:])
    names = [side_names[hops], across_names[hops], across_names[hops - 1]]
    blocks = [(side[hops][0], True, 0, 0, 0)]
    blocks += [(unit, False, 2, i, 0) for i, unit in enumerate(inner)]
    tasks = ((0, 0, (2,)), (1, 1, (0,)), (2, 2, (0,)))
    sums, (unit,) = row_sums(blocks, names, tasks, "end_terms", (0,), room=3)
    for half in range(2):
        total = total + moved(sums[1:], back(1 - hops, 1 - half))[half : half + 1]
    blocks = [(unit, False, 0, 0, 0), (facing, True, 1, 0, 0)]
    sums, (facing,) = row_sums(
        blocks, names, ((0, 0, (1,)),), "end_terms", (1,), before=sums[:END_ROOM], room=END_ROOM
    )
    total = total + moved(sums, back(hops))[:1]
    weight = in_vmem(weights_kernel, (rows, 2 * rows), jnp.bfloat16, "end_weights", *names)
    sums = in_vmem(
        last_kernel, (1, rows), jnp.float32, "last_terms", side[hops][1], facing, inner[1], weight
    )
    total = total + moved(sums, back(hops, 1))
    return jnp.log1p(total)[0]


def solution(mesh):
    return jax.shard_map(
        per_device,
        mesh=mesh,
        in_specs=(P(("groups", "blk"), None), P(("groups", "blk"), None), P("groups")),
        out_specs=P(("groups", "blk")),
        check_vma=False,
    )
```
